32 devices in a mesh: pipe: 4 (over x, core), dp: 2 (over y), tensor: 4 (over z).
Axes of the slice: x: 2, y: 2, z: 4, core: 2. Of those that a mesh axis runs over, the one named last changes fastest.
Arguments:
- tokens: bfloat16 [4, 512, 5120], P('pipe', 'dp', 'tensor'), may hold values from -6 to 6
- norm_gain: bfloat16 [4, 5120], P('pipe'), may hold values from 0.099609375 to 1.8984375
- w_query: bfloat16 [4, 5120, 4096], P('pipe', None, 'tensor'), may hold values from -0.078125 to 0.078125
- key_value_weight: bfloat16 [4, 5120, 1024], P('pipe', None, 'tensor'), may hold values from -0.078125 to 0.078125
- w_out: bfloat16 [4, 4096, 5120], P('pipe', 'tensor'), may hold values from -0.5 to 0.5
- cache_kv: bfloat16 [4, 2048, 4, 256], P('pipe', 'dp', 'tensor'), may hold values from -80 to 80
- cache_lengths: int32 [4, 4], P('pipe'), may hold values from 1 to 1024, 2048 in all within a row
- row_lengths: int32 [4, 4], P('pipe'), may hold values from 1 to 256, 512 in all within a row
- block_owner: int32 [4, 4, 1], P('pipe'), may hold values from 0 to 1; in each aligned block of 2 rows (0 to 1, 2 to 3, ..., all dimensions but the last counted through in order) no two rows name the same one
Outputs:
- handed: bfloat16 [4, 512, 5120], P('pipe', 'dp', 'tensor')
- blocks_held: float32 [4, 2], P('pipe', 'dp')
The draws below stay inside these ranges and needn't reach their ends.
Inputs may be any that keep to these rules, and one draw needn't show every extreme that they name: `block_owner`: the 2 aligned row blocks of one data rank at one section hand at most 1 block to any one data rank. `cache_lengths`: each section's documents hold 2048 cached positions in all; the longest exactly 1024. `row_lengths`: each section's documents hold 512 rows in all; the longest exactly 256.
All inputs are finite; a program needn't handle non-finite values.
Results may differ from the reference program's by a relative error of at most 0.012.
The reference program's roundings to bfloat16 on the way count: a program that leaves them out, or rounds other values in their place, can miss the bound.
Values may be sent and summed in bfloat16 or wider, within the bound.
No kernel may reach another device: no remote copies, remote signals or barrier semaphores. Data moves between devices by JAX's collectives and lax.ppermute only.
A program may use at most 192 MiB of HBM per device.

```python
import math
import jax
import jax.numpy as jnp
import numpy as np
from jax import lax

MODEL_WIDTH = 5120
QUERY_HEADS = 32
LOOKUP_CHANNELS = 4
HEAD_SIZE = 128
BLOCK_ROWS = 128
BLK_DEV = 2
NDOC = 4
HANDOVER_PARTS = 4
HQ_DEV = 8
NBLK = 4
MICRO_ROWS = 512
STORED_PLACES = 2048
CMAX = 1024
RMAX = 256
PAIR = 1
N_DP = 2
N_TENSOR = 4


def draw_cache_kv(key, part):
    key = jax.random.fold_in(key, 11)
    extent_size = (HANDOVER_PARTS, STORED_PLACES, LOOKUP_CHANNELS, 2 * HEAD_SIZE)
    key_one = jax.random.fold_in(key, 0)
    element_sequence = jnp.clip(jax.random.normal(key_one, extent_size, jnp.float32), -6.0, 6.0)
    return element_sequence.astype(jnp.bfloat16)


def shard_levels(key, shape, cuts, low, top_value):
    gain = 1.0
    for axis_at, shards_of in cuts:
        draws = jax.random.uniform(jax.random.fold_in(jax.random.fold_in(key, 6), axis_at), (shards_of,), jnp.float32, low / len(cuts), top_value / len(cuts))
        gain = gain * jnp.repeat(jnp.exp(draws), shape[axis_at] // shards_of).reshape((-1,) + (1,) * (len(shape) - 1 - axis_at))
    return gain


def profile(number_of, total, reach, skew):
    portions = [(1 << 20) // math.isqrt(grade ** skew) + 1 for grade in range(2, number_of + 1)]
    spare, given = total - reach - (number_of - 1), [1] * (number_of - 1)
    while spare > 0:
        movable = [i for i in range(number_of - 1) if given[i] < reach]
        pool, left = sum([portions[i] for i in movable]), spare
        for i in movable:
            extra = min(reach - given[i], max(1, left * portions[i] // pool), spare)
            given[i] = given[i] + extra
            spare = spare - extra
    return np.array([reach] + given)


def uneven(rng, count, total, most, skew):
    if count == 2:
        one = jax.random.randint(rng, (), max(1, total - most), min(most, total - 1) + 1)
        return jnp.stack([one, total - one])
    tallies = jnp.asarray(profile(count, total, most, skew), jnp.int32)
    pairs = (count - 1) // 2
    source_of, taker = tallies[1:1 + 2 * pairs:2], tallies[2:2 + 2 * pairs:2]
    slack = jnp.minimum(source_of - 1, most - taker)
    passed = jax.random.randint(jax.random.fold_in(rng, 1), (pairs,), 0, 1 << 20) % (slack + 1)
    tallies = tallies.at[1:1 + 2 * pairs:2].set(source_of - passed).at[2:2 + 2 * pairs:2].set(taker + passed)
    return tallies[jax.random.permutation(jax.random.fold_in(rng, 2), count)]


def routed_block(own_key, own, number, rows, count, top, limit, slope):
    order = jax.random.permutation(own_key, count)
    heavy_load, ordinary = portions_of(count, rows * top, limit, slope, True), portions_of(count, rows * top, limit, slope, False)
    places = jnp.arange(count)

    def named(sizes, turn):
        used = int((sizes > 0).sum())
        fixed = max(1, used // 4)
        moved = fixed + (places - fixed + turn * (used - fixed)) % max(1, count - fixed)
        return jnp.zeros((count,), jnp.int32).at[order[jnp.where(places < fixed, places, moved)]].set(jnp.asarray(sizes, jnp.int32))

    sizes = jnp.where(number % 4 == 0, named(heavy_load, number // 4), named(ordinary, number - number // 4 - 1))
    mixed = jax.random.permutation(jax.random.fold_in(own, 3), count)
    giver, receiver = mixed[0:count // 2 * 2:2], mixed[1:count // 2 * 2:2]
    margin = jnp.minimum(sizes[giver] - 1, limit - sizes[receiver]) // 2
    margin = jnp.where((giver == order[0]) | (receiver == order[0]) | (sizes[receiver] == 0), 0, jnp.maximum(margin, 0))
    moved = jax.random.randint(jax.random.fold_in(own, 4), (count // 2,), 0, 1 << 20) % (margin + 1)
    sizes = sizes.at[giver].add(-moved).at[receiver].add(moved)
    items = jnp.searchsorted(jnp.cumsum(sizes), jnp.arange(rows * top), side="right").astype(jnp.int32)
    grid = items.reshape(top, rows).T
    grid = grid[jax.random.permutation(jax.random.fold_in(own, 1), rows)]
    turn = jax.random.randint(jax.random.fold_in(own, 2), (rows, 1), 0, top)
    return jnp.take_along_axis(grid, (jnp.arange(top)[None, :] + turn) % top, axis=1)


def portions_of(count, total, bound, slope, full):
    portions = [(1 << 20) // math.isqrt(rank ** slope) + 1 for rank in range(1, count + 1)]
    largest = bound if full else min(bound, max(-(-total // count), total * portions[0] // sum(portions)))
    least = 1 if total - largest >= count - 1 else 0
    counts, rest = [largest] + [least] * (count - 1), total - largest - least * (count - 1)
    while rest > 0:
        free = [i for i in range(1, count) if counts[i] < largest] or [i for i in range(1, count) if counts[i] < bound]
        mass, remaining = sum([portions[i] for i in free]), rest
        for i in free:
            more = min(bound - counts[i], max(1, remaining * portions[i] // mass), rest)
            counts[i] = counts[i] + more
            rest = rest - more
    return np.array(counts)


def normal_values(key, dims, width, most, shards=(), kind=jnp.bfloat16):
    values = jax.random.normal(key, dims, jnp.float32) * width
    if len(shards) > 0:
        values = shard_levels(key, dims, shards, -0.22, 0.18) * values
    return jnp.clip(values, min=-most, max=most).astype(kind)


def setup_inputs(seed: int = 0) -> dict:
    keys = jax.random.split(jax.random.key(seed), 10)
    tokens = normal_values(keys[0], (HANDOVER_PARTS, MICRO_ROWS, MODEL_WIDTH), 1.0, 6.0, ((0, 4), (1, 2), (2, 4)))
    norm_gain = jnp.clip(1.0 + 0.18 * jax.random.normal(keys[1], (HANDOVER_PARTS, MODEL_WIDTH), jnp.float32), 0.099609375, 1.8984375).astype(jnp.bfloat16)
    w_query = normal_values(keys[2], (HANDOVER_PARTS, MODEL_WIDTH, QUERY_HEADS * HEAD_SIZE), MODEL_WIDTH ** -0.5, 0.078125, ((0, 4), (2, 4)))
    key_value_weight = normal_values(keys[3], (HANDOVER_PARTS, MODEL_WIDTH, LOOKUP_CHANNELS * 2 * HEAD_SIZE), MODEL_WIDTH ** -0.5, 0.078125, ((0, 4), (2, 4)))
    w_out = normal_values(keys[4], (HANDOVER_PARTS, QUERY_HEADS * HEAD_SIZE, MODEL_WIDTH), HEAD_SIZE ** -0.5, 0.5, ((0, 4), (1, 4)))
    cache_kv = draw_cache_kv(jax.random.fold_in(keys[9], 71), 0)
    cache_lengths = jax.vmap(lambda own: uneven(own, NDOC, STORED_PLACES, CMAX, 2))(jax.random.split(keys[6], HANDOVER_PARTS)).reshape((HANDOVER_PARTS, NDOC)).astype(jnp.int32)
    row_lengths = jax.vmap(lambda own: uneven(own, NDOC, MICRO_ROWS, RMAX, 2))(jax.random.split(keys[7], HANDOVER_PARTS)).reshape((HANDOVER_PARTS, NDOC)).astype(jnp.int32)
    block_owner_keys = jax.random.split(jax.random.fold_in(keys[8], 1), HANDOVER_PARTS * NBLK // BLK_DEV)
    block_owner_turns = jax.random.permutation(jax.random.fold_in(keys[8], 3), HANDOVER_PARTS * NBLK // BLK_DEV)
    block_owner = jax.vmap(lambda own, number: routed_block(jax.random.fold_in(keys[8], 2), own, number, BLK_DEV, N_DP, 1, PAIR, 2))(block_owner_keys, block_owner_turns).reshape((HANDOVER_PARTS, NBLK, 1))
    return {"tokens": tokens, "norm_gain": norm_gain, "w_query": w_query, "key_value_weight": key_value_weight, "w_out": w_out, "cache_kv": cache_kv, "cache_lengths": cache_lengths, "row_lengths": row_lengths, "block_owner": block_owner}


EPS = 1e-06
NEG = -1e+30

def doc_ids(lengths, amount):
    bounds = jnp.cumsum(lengths).astype(jnp.int32)
    places = jnp.arange(amount, dtype=jnp.int32)
    return lax.optimization_barrier(jnp.sum((places[:, None] >= bounds[None, :]).astype(jnp.int32), axis=1))

def block_loads(row_len, cache_len, amount, block_size):
    row_doc = doc_ids(row_len, amount)
    bounds = jnp.cumsum(row_len).astype(jnp.int32)
    starts = bounds - row_len.astype(jnp.int32)
    offsets = cache_len.astype(jnp.int32) - starts + 1
    doc_numbers = jnp.arange(row_len.shape[0], dtype=jnp.int32)
    matches = (row_doc[:, None] == doc_numbers[None, :]).astype(jnp.int32)
    per_row = lax.optimization_barrier(jnp.sum(matches * offsets[None, :], axis=1)) + jnp.arange(amount, dtype=jnp.int32)
    return lax.optimization_barrier(jnp.sum(per_row.reshape(amount // block_size, block_size), axis=1))

def run_section(inputs, gain_row, query_weight, keyval_weight, out_weight, cached_rows, cache_len, row_len):
    widened = inputs.astype(jnp.float32)
    factor = lax.rsqrt(lax.optimization_barrier(jnp.mean(widened * widened, axis=1, keepdims=True)) + EPS)
    normed = (widened * factor * gain_row.astype(jnp.float32)).astype(jnp.bfloat16)
    query_rows = jnp.dot(normed, query_weight, preferred_element_type=jnp.float32).astype(jnp.bfloat16)
    key_value_rows = jnp.dot(normed, keyval_weight, preferred_element_type=jnp.float32).astype(jnp.bfloat16)
    history_rows = jnp.concatenate([cached_rows.reshape(STORED_PLACES, LOOKUP_CHANNELS * 2 * HEAD_SIZE), key_value_rows], axis=0)
    history_rows = history_rows.reshape(STORED_PLACES + MICRO_ROWS, LOOKUP_CHANNELS, 2 * HEAD_SIZE)
    key_part = history_rows[:, :, :HEAD_SIZE].astype(jnp.float32)
    value_part = history_rows[:, :, HEAD_SIZE:].astype(jnp.float32)
    cache_doc = doc_ids(cache_len, STORED_PLACES)
    row_doc = doc_ids(row_len, MICRO_ROWS)
    key_doc = jnp.concatenate([cache_doc, row_doc])
    key_row = jnp.concatenate([jnp.full((STORED_PLACES,), -1, jnp.int32), jnp.arange(MICRO_ROWS, dtype=jnp.int32)])
    group_list = QUERY_HEADS // LOOKUP_CHANNELS
    query_row_blocks = query_rows.reshape(MICRO_ROWS // BLOCK_ROWS, BLOCK_ROWS, LOOKUP_CHANNELS, group_list, HEAD_SIZE)

    def one_block(packed):
        block_query, block_index = packed
        start_row = (block_index * BLOCK_ROWS).astype(jnp.int32)
        own_rows = start_row + jnp.arange(BLOCK_ROWS, dtype=jnp.int32)
        own_docs = lax.dynamic_slice(row_doc, (start_row,), (BLOCK_ROWS,))
        visible = (own_docs[:, None] == key_doc[None, :]) & (key_row[None, :] <= own_rows[:, None])
        visible_wide = visible[:, None, None, :]
        scores = jnp.einsum('qkgd,nkd->qkgn', block_query.astype(jnp.float32), key_part) * HEAD_SIZE ** (-0.5)
        scores = jnp.where(visible_wide, scores, NEG)
        highest = lax.optimization_barrier(jnp.max(scores, axis=3, keepdims=True))
        weights = jnp.where(visible_wide, jnp.exp(scores - highest), 0.0)
        totals = lax.optimization_barrier(jnp.sum(weights, axis=3))
        rounded = lax.optimization_barrier(weights.astype(jnp.bfloat16)).astype(jnp.float32)
        summed = jnp.einsum('qkgn,nkd->qkgd', rounded, value_part)
        return (summed / totals[..., None]).astype(jnp.bfloat16)
    block_numbers = jnp.arange(MICRO_ROWS // BLOCK_ROWS, dtype=jnp.int32)
    attended = lax.map(one_block, (query_row_blocks, block_numbers)).reshape(MICRO_ROWS, QUERY_HEADS * HEAD_SIZE)
    head_width = HQ_DEV * HEAD_SIZE
    partial_sum = jnp.zeros((MICRO_ROWS, MODEL_WIDTH), jnp.float32)
    for group_index in range(N_TENSOR):
        lower = group_index * head_width
        product = jnp.dot(attended[:, lower:lower + head_width], out_weight[lower:lower + head_width], preferred_element_type=jnp.float32)
        partial_sum = partial_sum + lax.optimization_barrier(product.astype(jnp.bfloat16)).astype(jnp.float32)
    return (widened + partial_sum).astype(jnp.bfloat16)

def reference(tokens, norm_gain, w_query, key_value_weight, w_out, cache_kv, cache_lengths, row_lengths, block_owner):
    results = []
    for section_index in range(HANDOVER_PARTS):
        results.append(run_section(tokens[section_index], norm_gain[section_index], w_query[section_index], key_value_weight[section_index], w_out[section_index], cache_kv[section_index], cache_lengths[section_index], row_lengths[section_index]))
    handed = jnp.stack([results[(section_index - 1) % HANDOVER_PARTS] for section_index in range(HANDOVER_PARTS)])
    rank_ids = jnp.arange(N_DP, dtype=jnp.int32)
    loads = jnp.stack([block_loads(row_lengths[section_index], cache_lengths[section_index], MICRO_ROWS, BLOCK_ROWS) for section_index in range(HANDOVER_PARTS)])
    matched = (block_owner[:, :, 0][:, :, None] == rank_ids[None, None, :]).astype(jnp.int32)
    work_sum = lax.optimization_barrier(jnp.sum(matched * loads[:, :, None], axis=1))
    blocks_held = work_sum.astype(jnp.float32) / jnp.float32(BLOCK_ROWS * (CMAX + RMAX))
    return (handed, blocks_held)
```

```python
import functools

import jax
import jax.numpy as jnp
from jax import lax
from jax.experimental import pallas as pl
from jax.experimental.pallas import tpu as pltpu
from jax.sharding import PartitionSpec as P

HEAD_SIZE = 128
BLOCK_ROWS = 128
EPS = 1e-06
NEG = -1e30
LOG2E = 1.4426950408889634
MIB = 1024 * 1024
SCORE_BYTES = 13 * MIB
PARTS = 4
WEIGHT_CUTS = 4
KEY_TILE = 384


def swap(block, axis, pairs):
    return lax.ppermute(block, axis, pairs)


def xor_pairs(count, mask, among=None):
    return [(i, i ^ mask) for i in range(count) if among is None or i in among]


def after(value, *others):
    return lax.optimization_barrier((value, *others))[0]


def in_vmem(x):
    return pltpu.with_memory_space_constraint(x, pltpu.VMEM)


def in_hbm(x):
    return pltpu.with_memory_space_constraint(x, pltpu.HBM)


def resident(kernel, name, outs, args, scalars=(), weights=(), scratch=(), limit=16, moved=0):
    spaces = [pl.BlockSpec(memory_space=pltpu.SMEM)] * len(scalars)
    spaces += [pl.BlockSpec(memory_space=pltpu.VMEM)] * len(args)
    spaces += [pl.BlockSpec(memory_space=pl.ANY)] * len(weights)
    return pl.pallas_call(
        kernel,
        in_specs=spaces,
        out_specs=[pl.BlockSpec(memory_space=pltpu.VMEM)] * len(outs),
        out_shape=[
            jax.ShapeDtypeStruct(shape, dtype) if shape == (1, 1) else pltpu.VMEM(shape, dtype)
            for shape, dtype in outs
        ],
        scratch_shapes=list(scratch),
        compiler_params=pltpu.CompilerParams(vmem_limit_bytes=limit * MIB),
        cost_estimate=pl.CostEstimate(flops=0, bytes_accessed=moved, transcendentals=0),
        name=name,
    )(*scalars, *[in_vmem(x) for x in args], *[in_hbm(w) for w in weights])


def start_copies(copies):
    for copy in copies:
        copy.start()


def wait_copies(copies):
    for copy in copies:
        copy.wait()


def row_copies(w_ref, start, held, sems):
    cuts = sems.shape[0]
    rows = held.shape[0] // cuts
    return [
        pltpu.make_async_copy(
            w_ref.at[pl.ds(pl.multiple_of(start + at * rows, 16), rows)],
            held.at[pl.ds(at * rows, rows)],
            sems.at[at],
        )
        for at in range(cuts)
    ]


def column_copies(w_ref, start, held, sems):
    cuts = sems.shape[0]
    rows, width = held.shape
    rows = rows // cuts
    return [
        pltpu.make_async_copy(
            w_ref.at[pl.ds(at * rows, rows), pl.ds(pl.multiple_of(start, 128), width)],
            held.at[pl.ds(at * rows, rows)],
            sems.at[at],
        )
        for at in range(cuts)
    ]


def store_normed(out_ref, x_ref, factor_ref, gain_ref, place):
    width = x_ref.shape[1]
    gain = gain_ref[:, pl.ds(pl.multiple_of(place * width, 128), width)].astype(jnp.float32)
    for c in range(0, width, 128):
        wide = x_ref[:, c : c + 128].astype(jnp.float32)
        out_ref[:, c : c + 128] = (wide * factor_ref[...] * gain[:, c : c + 128]).astype(jnp.bfloat16)


def documents(lengths, docs):
    starts, ends, last = [], [], jnp.int32(0)
    for d in range(docs):
        starts.append(last)
        last = last + lengths[0, d]
        ends.append(last)
    return starts, ends


def early_kernel(
    own, near, far, rest_ref, gain_ref, wq_ref, wkv_ref,
    q_ref, kv_ref, factor_ref, wq_held, wkv_held, normed, sems_q, sems_kv,
):
    place = lax.axis_index("tensor")
    width = own.shape[1]
    shards = (own, near, far)
    copies = []
    for at in range(len(shards)):
        first, spot = (place ^ at) * width, pl.ds(at * width, width)
        copies += row_copies(wkv_ref, first, wkv_held.at[spot], sems_kv.at[at])
        copies += row_copies(wq_ref, first, wq_held.at[spot], sems_q.at[at])
    start_copies(copies)
    squares = rest_ref[:, :1]
    for x_ref in shards:
        wide = x_ref[...].astype(jnp.float32)
        squares += jnp.sum(wide * wide, axis=1, keepdims=True)
    factor = lax.rsqrt(squares / (width * (len(shards) + 1)) + EPS)
    factor_ref[...] = jnp.broadcast_to(factor, factor_ref.shape)
    for at, x_ref in enumerate(shards):
        store_normed(normed.at[:, pl.ds(at * width, width)], x_ref, factor_ref, gain_ref, place ^ at)
    wait_copies(copies)
    kv_ref[...] = jnp.dot(normed[...], wkv_held[...], preferred_element_type=jnp.float32)
    q_ref[...] = jnp.dot(normed[...], wq_held[...], preferred_element_type=jnp.float32)


def early_projection(own, near, far, rest, gain, wq, wkv):
    rows, width = own.shape
    heads, kv_width = wq.shape[1], wkv.shape[1]
    return resident(
        early_kernel,
        "early_projection",
        [((rows, heads), jnp.float32), ((rows, kv_width), jnp.float32), ((rows, 128), jnp.float32)],
        [own, near, far, rest, gain],
        weights=[wq, wkv],
        scratch=[
            pltpu.VMEM((3 * width, heads), jnp.bfloat16),
            pltpu.VMEM((3 * width, kv_width), jnp.bfloat16),
            pltpu.VMEM((rows, 3 * width), jnp.bfloat16),
            pltpu.SemaphoreType.DMA((3, WEIGHT_CUTS)),
            pltpu.SemaphoreType.DMA((3, 1)),
        ],
        limit=24,
    )


def last_kv_kernel(
    cross, relayed, factor_ref, gain_ref, acc_ref, w_ref, kv_ref, normed, w_held, x, sems
):
    place = lax.axis_index("tensor")
    copies = row_copies(w_ref, (place ^ 3) * x.shape[1], w_held, sems)
    start_copies(copies)
    is_inner = (place > 0) & (place < PARTS - 1)

    @pl.when(is_inner)
    def _():
        store_normed(normed, cross, factor_ref, gain_ref, place ^ 3)

    @pl.when(jnp.logical_not(is_inner))
    def _():
        store_normed(normed, relayed, factor_ref, gain_ref, place ^ 3)

    wait_copies(copies)
    part = jnp.dot(normed[...], w_held[...], preferred_element_type=jnp.float32)
    kv_ref[...] = (acc_ref[...] + part).astype(jnp.bfloat16)


def last_kv(cross, relayed, factor, gain, acc, w):
    rows, columns = acc.shape
    width = relayed.shape[1]
    return resident(
        last_kv_kernel,
        "last_kv",
        [((rows, columns), jnp.bfloat16), ((rows, width), jnp.bfloat16)],
        [cross, relayed, factor, gain, acc],
        weights=[w],
        scratch=[
            pltpu.VMEM((width, columns), jnp.bfloat16),
            pltpu.VMEM((rows, width), jnp.bfloat16),
            pltpu.SemaphoreType.DMA((2,)),
        ],
        limit=8,
    )


def last_q_kernel(normed, acc_ref, w_ref, q_ref, w_held, sems):
    place = lax.axis_index("tensor")
    copies = row_copies(w_ref, (place ^ 3) * normed.shape[1], w_held, sems)
    start_copies(copies)
    wait_copies(copies)
    part = jnp.dot(normed[...], w_held[...], preferred_element_type=jnp.float32)
    q_ref[...] = (acc_ref[...] + part).astype(jnp.bfloat16)


def last_q(normed, acc, w):
    rows, width = normed.shape
    columns = w.shape[1]
    return resident(
        last_q_kernel,
        "last_q",
        [((rows, columns), jnp.bfloat16)],
        [normed, acc],
        weights=[w],
        scratch=[pltpu.VMEM((width, columns), jnp.bfloat16), pltpu.SemaphoreType.DMA((WEIGHT_CUTS,))],
        limit=8,
    )[0]


def attend_kernel(
    row_lengths, cache_lengths, owners, *refs, count, places, sub_rows, heads, tile, divisor
):
    cache, pieces = refs[0], refs[1 : 1 + count]
    q_ref, w_ref, attended_rows, part_ref, held_ref = refs[1 + count : 6 + count]
    w_held, fresh, scores, top, total, acc, sems, w_sems = refs[6 + count :]
    rank = lax.axis_index("dp")
    place = lax.axis_index("tensor")
    row_count = q_ref.shape[0]
    width = part_ref.shape[1]
    docs = row_lengths.shape[1]
    copies = []
    for at, (piece, own) in enumerate(zip(pieces, places)):
        size = piece.shape[0]
        start = 0 if own is None else (rank if own else 1 - rank) * size
        target = fresh.at[pl.ds(pl.multiple_of(start, 16), size)]
        copies.append(pltpu.make_async_copy(piece, target, sems.at[at]))
    w_copies = column_copies(w_ref, (place ^ 3) * width, w_held, w_sems)
    start_copies(copies + w_copies)

    row_start, row_end = documents(row_lengths, docs)
    cache_start, cache_end = documents(cache_lengths, docs)
    stacked = heads * sub_rows
    lanes = 128

    def by_doc(row, values):
        found = values[0]
        for d in range(1, docs):
            found = jnp.where(row >= row_start[d], values[d], found)
        return found

    pairs = jnp.int32(0)
    for block in range(owners.shape[1]):
        found = jnp.int32(0)
        for d in range(docs):
            low = jnp.maximum(row_start[d], block * BLOCK_ROWS)
            high = jnp.maximum(jnp.minimum(row_end[d], (block + 1) * BLOCK_ROWS), low)
            amount = high - low
            found += amount * (cache_lengths[0, d] + 1 - row_start[d])
            found += lax.shift_right_arithmetic((low + high - 1) * amount, 1)
        pairs += jnp.where(owners[0, block] == rank, found, 0)
    held_ref[...] = jnp.full(held_ref.shape, pairs, jnp.int32).astype(jnp.float32) / divisor

    def span(start, end):
        start = lax.div(start, 16) * 16
        return start, lax.div(end - start + tile - 1, tile)

    def tile_start(source, first, t):
        start = first + t * tile
        return start, pl.multiple_of(jnp.minimum(start, source.shape[0] - tile), 16)

    for step in range(row_count // sub_rows):
        spots = slice(step * sub_rows, (step + 1) * sub_rows)
        first_row = rank * row_count + step * sub_rows
        last_row = first_row + sub_rows - 1
        rows = first_row + lax.broadcasted_iota(jnp.int32, (sub_rows, 1), 0)
        queries = jnp.concatenate(
            [q_ref[spots, h * HEAD_SIZE : (h + 1) * HEAD_SIZE] for h in range(heads)], axis=0
        )
        top[...] = jnp.full(top.shape, NEG, jnp.float32)
        total[...] = jnp.zeros(total.shape, jnp.float32)
        acc[...] = jnp.zeros(acc.shape, jnp.float32)

        def score(source, first, base, low, high):
            def body(t, _):
                begin, start = tile_start(source, first, t)
                found = lax.dot_general(
                    queries,
                    source[pl.ds(start, tile), :HEAD_SIZE],
                    (((1,), (1,)), ((), ())),
                    preferred_element_type=jnp.float32,
                )
                spot = start + lax.broadcasted_iota(jnp.int32, (1, tile), 1)
                seen = (spot >= jnp.maximum(low, begin)) & (spot < high)
                found = jnp.where(seen[None], found.reshape(heads, sub_rows, tile), NEG)
                found = found.reshape(stacked, tile)
                scores[base + t] = found
                best = found[:, :lanes]
                for c in range(1, tile // lanes):
                    best = jnp.maximum(best, found[:, c * lanes : (c + 1) * lanes])
                top[...] = jnp.maximum(top[...], best)
                return 0

            return body

        cache_from, cache_tiles = span(by_doc(first_row, cache_start), by_doc(last_row, cache_end))
        new_from, new_tiles = span(by_doc(first_row, row_start), last_row + 1)
        low, high = by_doc(rows, cache_start), by_doc(rows, cache_end)
        lax.fori_loop(0, cache_tiles, score(cache, cache_from, 0, low, high), 0)
        if step == 0:
            wait_copies(copies)
        low, high = by_doc(rows, row_start), rows + 1
        lax.fori_loop(0, new_tiles, score(fresh, new_from, cache_tiles, low, high), 0)
        highest = jnp.max(top[...], axis=1, keepdims=True)

        def weigh(source, first, base):
            def body(t, _):
                _, start = tile_start(source, first, t)
                weights = jnp.exp2((scores[base + t] - highest) * (HEAD_SIZE**-0.5 * LOG2E))
                part = weights[:, :lanes]
                for c in range(1, tile // lanes):
                    part = part + weights[:, c * lanes : (c + 1) * lanes]
                total[...] += part
                acc[...] += jnp.dot(
                    weights.astype(jnp.bfloat16),
                    source[pl.ds(start, tile), HEAD_SIZE:],
                    preferred_element_type=jnp.float32,
                )
                return 0

            return body

        lax.fori_loop(0, cache_tiles, weigh(cache, cache_from, 0), 0)
        lax.fori_loop(0, new_tiles, weigh(fresh, new_from, cache_tiles), 0)
        attended = (acc[...] / jnp.sum(total[...], axis=1, keepdims=True)).astype(jnp.bfloat16)
        for h in range(heads):
            attended_rows[spots, h * HEAD_SIZE : (h + 1) * HEAD_SIZE] = attended[
                h * sub_rows : (h + 1) * sub_rows
            ]
    wait_copies(w_copies)
    part_ref[...] = jnp.dot(
        attended_rows[...], w_held[...], preferred_element_type=jnp.float32
    ).astype(jnp.bfloat16)


def attention(scalars, queries, cache, pieces, places, fresh, w, divisor):
    rows, width = queries.shape
    heads = width // HEAD_SIZE
    tiles = sum(pl.cdiv(amount, KEY_TILE) for amount in (cache.shape[0], fresh))
    sub_rows = BLOCK_ROWS
    while sub_rows > 32 and heads * sub_rows * tiles * KEY_TILE * 4 > SCORE_BYTES:
        sub_rows //= 2
    stacked = heads * sub_rows
    out_width = w.shape[1] // PARTS
    return resident(
        functools.partial(
            attend_kernel,
            count=len(pieces),
            places=places,
            sub_rows=sub_rows,
            heads=heads,
            tile=KEY_TILE,
            divisor=divisor,
        ),
        "attention",
        [((rows, width), jnp.bfloat16), ((rows, out_width), jnp.bfloat16), ((1, 1), jnp.float32)],
        [cache, *pieces, queries],
        scalars,
        weights=[w],
        scratch=[
            pltpu.VMEM((width, out_width), jnp.bfloat16),
            pltpu.VMEM((fresh, 2 * HEAD_SIZE), jnp.bfloat16),
            pltpu.VMEM((tiles, stacked, KEY_TILE), jnp.float32),
            pltpu.VMEM((stacked, 128), jnp.float32),
            pltpu.VMEM((stacked, 128), jnp.float32),
            pltpu.VMEM((stacked, HEAD_SIZE), jnp.float32),
            pltpu.SemaphoreType.DMA((len(pieces),)),
            pltpu.SemaphoreType.DMA((WEIGHT_CUTS,)),
        ],
        limit=26,
        moved=2 * w.size,
    )


def out_kernel(a_ref, w_ref, *refs, masks):
    outs, (w_held, sems) = refs[: len(masks)], refs[len(masks) :]
    place = lax.axis_index("tensor")
    width = outs[0].shape[1]
    copies = [
        column_copies(w_ref, (place ^ mask) * width, w_held.at[at], sems.at[at])
        for at, mask in enumerate(masks)
    ]
    for some in copies:
        start_copies(some)
    for at, out_ref in enumerate(outs):
        wait_copies(copies[at])
        out_ref[...] = jnp.dot(
            a_ref[...], w_held[at], preferred_element_type=jnp.float32
        ).astype(jnp.bfloat16)


def out_projection(attended, w, masks):
    rows, depth = attended.shape
    width = w.shape[1] // PARTS
    return resident(
        functools.partial(out_kernel, masks=masks),
        "out_projection",
        [((rows, width), jnp.bfloat16)] * len(masks),
        [attended],
        weights=[w],
        scratch=[
            pltpu.VMEM((len(masks), depth, width), jnp.bfloat16),
            pltpu.SemaphoreType.DMA((len(masks), WEIGHT_CUTS)),
        ],
        limit=16,
    )


def on_device(
    tokens, norm_gain, w_query, key_value_weight, w_out, cache_kv, cache_lengths, row_lengths, block_owner
):
    ranks = lax.axis_size("dp")
    splits = lax.axis_size("tensor")
    sections = lax.axis_size("pipe")
    rank = lax.axis_index("dp")
    own = tokens[0]
    row_count = own.shape[0]
    cache_rows = cache_kv.shape[1]
    gain, wq, wkv, wo = norm_gain, w_query[0], key_value_weight[0], w_out[0]
    assert splits == PARTS and row_count % BLOCK_ROWS == 0
    inner_pairs = xor_pairs(splits, 3, range(1, splits - 1))
    pair = [(0, 1), (1, 0)] if ranks == 2 else None

    def onwards(block, pairs):
        route = [
            (p * splits + a, (p + 1) % sections * splits + b) for p in range(sections) for a, b in pairs
        ]
        return swap(block, ("pipe", "tensor"), route)

    far = swap(own, "tensor", xor_pairs(splits, 2))
    near = swap(own, "tensor", xor_pairs(splits, 1))
    square = jnp.sum(jnp.square(own.astype(jnp.float32)), axis=1)[None]
    rest = swap(square, "tensor", xor_pairs(splits, 3))
    cross = swap(own, "tensor", inner_pairs)
    far, near, rest = lax.optimization_barrier((far, near, rest))
    relayed = swap(far, "tensor", [(1, 0), (2, 3)])
    cache = after(cache_kv.reshape(cache_rows, 2 * HEAD_SIZE), far)
    if pair:
        other = swap(cache, "dp", pair)
        cache = jnp.where(
            rank == 0, jnp.concatenate([cache, other]), jnp.concatenate([other, cache])
        )
    else:
        cache = lax.all_gather(cache, "dp", axis=0, tiled=True)

    rest = jnp.broadcast_to(rest[0][:, None], (row_count, 128))
    divisor = BLOCK_ROWS * (cache_rows * ranks // 2 + row_count * ranks // 2)
    early_q, early_kv, factor = early_projection(own, near, far, rest, gain, wq, wkv)
    kv, normed = last_kv(cross, relayed, factor, gain, early_kv, wkv)
    if pair:
        pieces, places = [kv, swap(kv, "dp", pair)], (1, 0)
    else:
        pieces, places = [lax.all_gather(kv, "dp", axis=0, tiled=True)], (None,)
    queries = last_q(normed, early_q, wq)
    home = onwards(after(own, kv), xor_pairs(splits, 0))

    scalars = (row_lengths, cache_lengths, block_owner[:, :, 0])
    attended, third, blocks_held = attention(
        scalars, queries, cache, pieces, places, ranks * row_count, wo, float(divisor)
    )
    from_outer = swap(third, "tensor", [(0, 1), (3, 2)])
    from_cross = onwards(third, inner_pairs)
    attended, home = lax.optimization_barrier((attended, home))
    second, first, same = out_projection(attended, wo, (2, 1, 0))
    from_far = onwards(second, [(0, 2), (3, 1)])
    summed = (second.astype(jnp.float32) + from_outer.astype(jnp.float32)).astype(jnp.bfloat16)
    first, same, summed = lax.optimization_barrier((first, same, summed))
    from_near = onwards(first, xor_pairs(splits, 1))
    from_same = onwards(same, xor_pairs(splits, 0))
    from_sum = onwards(summed, [(1, 3), (2, 0)])
    total = from_same.astype(jnp.float32)
    for block in (from_near, from_far, from_cross, from_sum):
        total = total + block.astype(jnp.float32)
    handed = (home.astype(jnp.float32) + total).astype(jnp.bfloat16)[None]
    return handed, blocks_held


def solution(mesh):
    placed = (
        P("pipe", "dp", "tensor"),
        P("pipe", None),
        P("pipe", None, "tensor"),
        P("pipe", None, "tensor"),
        P("pipe", "tensor", None),
        P("pipe", "dp", "tensor", None),
        P("pipe", None),
        P("pipe", None),
        P("pipe", None, None),
    )
    return jax.shard_map(
        on_device,
        mesh=mesh,
        in_specs=placed,
        out_specs=(P("pipe", "dp", "tensor"), P("pipe", "dp")),
        check_vma=False,
    )
```

```python
import functools

import jax
import jax.numpy as jnp
from jax import lax
from jax.experimental import pallas as pl
from jax.experimental.pallas import tpu as pltpu
from jax.sharding import PartitionSpec as P

HEAD_SIZE = 128
BLOCK_ROWS = 128
EPS = 1e-06
NEG = -1e30
LOG2E = 1.4426950408889634
MIB = 1024 * 1024
SCORE_BYTES = 13 * MIB
PARTS = 4
WEIGHT_CUTS = 4
KEY_TILE = 384


def swap(block, axis, pairs):
    return lax.ppermute(block, axis, pairs)


def xor_pairs(count, mask, among=None):
    return [(i, i ^ mask) for i in range(count) if among is None or i in among]


def after(value, *others):
    return lax.optimization_barrier((value, *others))[0]


def in_vmem(x):
    return pltpu.with_memory_space_constraint(x, pltpu.VMEM)


def in_hbm(x):
    return pltpu.with_memory_space_constraint(x, pltpu.HBM)


def resident(kernel, name, outs, args, scalars=(), weights=(), scratch=(), limit=16, moved=0):
    spaces = [pl.BlockSpec(memory_space=pltpu.SMEM)] * len(scalars)
    spaces += [pl.BlockSpec(memory_space=pltpu.VMEM)] * len(args)
    spaces += [pl.BlockSpec(memory_space=pl.ANY)] * len(weights)
    return pl.pallas_call(
        kernel,
        in_specs=spaces,
        out_specs=[pl.BlockSpec(memory_space=pltpu.VMEM)] * len(outs),
        out_shape=[
            jax.ShapeDtypeStruct(shape, dtype) if shape == (1, 1) else pltpu.VMEM(shape, dtype)
            for shape, dtype in outs
        ],
        scratch_shapes=list(scratch),
        compiler_params=pltpu.CompilerParams(vmem_limit_bytes=limit * MIB),
        cost_estimate=pl.CostEstimate(flops=0, bytes_accessed=moved, transcendentals=0),
        name=name,
    )(*scalars, *[in_vmem(x) for x in args], *[in_hbm(w) for w in weights])


def start_copies(copies):
    for copy in copies:
        copy.start()


def wait_copies(copies):
    for copy in copies:
        copy.wait()


def row_copies(w_ref, start, held, sems):
    cuts = sems.shape[0]
    rows = held.shape[0] // cuts
    return [
        pltpu.make_async_copy(
            w_ref.at[pl.ds(pl.multiple_of(start + at * rows, 16), rows)],
            held.at[pl.ds(at * rows, rows)],
            sems.at[at],
        )
        for at in range(cuts)
    ]


def column_copies(w_ref, start, held, sems):
    cuts = sems.shape[0]
    rows, width = held.shape
    rows = rows // cuts
    return [
        pltpu.make_async_copy(
            w_ref.at[pl.ds(at * rows, rows), pl.ds(pl.multiple_of(start, 128), width)],
            held.at[pl.ds(at * rows, rows)],
            sems.at[at],
        )
        for at in range(cuts)
    ]


def store_normed(out_ref, x_ref, factor_ref, gain_ref, place):
    width = x_ref.shape[1]
    gain = gain_ref[:, pl.ds(pl.multiple_of(place * width, 128), width)].astype(jnp.float32)
    for c in range(0, width, 128):
        wide = x_ref[:, c : c + 128].astype(jnp.float32)
        out_ref[:, c : c + 128] = (wide * factor_ref[...] * gain[:, c : c + 128]).astype(jnp.bfloat16)


def documents(lengths, docs):
    starts, ends, last = [], [], jnp.int32(0)
    for d in range(docs):
        starts.append(last)
        last = last + lengths[0, d]
        ends.append(last)
    return starts, ends


def by_position(place, for_inner, for_outer):
    return jnp.where((place > 0) & (place < PARTS - 1), for_inner, for_outer)


def early_kernel(
    own, one, two, rest_ref, gain_ref, wq_ref, wkv_ref,
    q_ref, kv_ref, factor_ref, wq_held, wkv_held, normed, sems_q, sems_kv,
):
    place = lax.axis_index("tensor")
    width = own.shape[1]
    shards = (own, one, two)
    spots = (place, place ^ by_position(place, 2, 1), place ^ by_position(place, 1, 2))
    copies = []
    for at in range(len(shards)):
        first, spot = spots[at] * width, pl.ds(at * width, width)
        copies += row_copies(wkv_ref, first, wkv_held.at[spot], sems_kv.at[at])
        copies += row_copies(wq_ref, first, wq_held.at[spot], sems_q.at[at])
    start_copies(copies)
    squares = rest_ref[:, :1]
    for x_ref in shards:
        wide = x_ref[...].astype(jnp.float32)
        squares += jnp.sum(wide * wide, axis=1, keepdims=True)
    factor = lax.rsqrt(squares / (width * (len(shards) + 1)) + EPS)
    factor_ref[...] = jnp.broadcast_to(factor, factor_ref.shape)
    for at, x_ref in enumerate(shards):
        store_normed(normed.at[:, pl.ds(at * width, width)], x_ref, factor_ref, gain_ref, spots[at])
    wait_copies(copies)
    kv_ref[...] = jnp.dot(normed[...], wkv_held[...], preferred_element_type=jnp.float32)
    q_ref[...] = jnp.dot(normed[...], wq_held[...], preferred_element_type=jnp.float32)


def early_projection(own, one, two, rest, gain, wq, wkv):
    rows, width = own.shape
    heads, kv_width = wq.shape[1], wkv.shape[1]
    return resident(
        early_kernel,
        "early_projection",
        [((rows, heads), jnp.float32), ((rows, kv_width), jnp.float32), ((rows, 128), jnp.float32)],
        [own, one, two, rest, gain],
        weights=[wq, wkv],
        scratch=[
            pltpu.VMEM((3 * width, heads), jnp.bfloat16),
            pltpu.VMEM((3 * width, kv_width), jnp.bfloat16),
            pltpu.VMEM((rows, 3 * width), jnp.bfloat16),
            pltpu.SemaphoreType.DMA((3, WEIGHT_CUTS)),
            pltpu.SemaphoreType.DMA((3, 1)),
        ],
        limit=24,
    )


def last_kv_kernel(
    cross, relayed, factor_ref, gain_ref, acc_ref, w_ref, kv_ref, normed, w_held, x, sems
):
    place = lax.axis_index("tensor")
    copies = row_copies(w_ref, (place ^ 3) * x.shape[1], w_held, sems)
    start_copies(copies)
    is_inner = (place > 0) & (place < PARTS - 1)

    @pl.when(is_inner)
    def _():
        store_normed(normed, cross, factor_ref, gain_ref, place ^ 3)

    @pl.when(jnp.logical_not(is_inner))
    def _():
        store_normed(normed, relayed, factor_ref, gain_ref, place ^ 3)

    wait_copies(copies)
    part = jnp.dot(normed[...], w_held[...], preferred_element_type=jnp.float32)
    kv_ref[...] = (acc_ref[...] + part).astype(jnp.bfloat16)


def last_kv(cross, relayed, factor, gain, acc, w):
    rows, columns = acc.shape
    width = relayed.shape[1]
    return resident(
        last_kv_kernel,
        "last_kv",
        [((rows, columns), jnp.bfloat16), ((rows, width), jnp.bfloat16)],
        [cross, relayed, factor, gain, acc],
        weights=[w],
        scratch=[
            pltpu.VMEM((width, columns), jnp.bfloat16),
            pltpu.VMEM((rows, width), jnp.bfloat16),
            pltpu.SemaphoreType.DMA((2,)),
        ],
        limit=8,
    )


def last_q_kernel(normed, acc_ref, w_ref, q_ref, w_held, sems):
    place = lax.axis_index("tensor")
    copies = row_copies(w_ref, (place ^ 3) * normed.shape[1], w_held, sems)
    start_copies(copies)
    wait_copies(copies)
    part = jnp.dot(normed[...], w_held[...], preferred_element_type=jnp.float32)
    q_ref[...] = (acc_ref[...] + part).astype(jnp.bfloat16)


def last_q(normed, acc, w):
    rows, width = normed.shape
    columns = w.shape[1]
    return resident(
        last_q_kernel,
        "last_q",
        [((rows, columns), jnp.bfloat16)],
        [normed, acc],
        weights=[w],
        scratch=[pltpu.VMEM((width, columns), jnp.bfloat16), pltpu.SemaphoreType.DMA((WEIGHT_CUTS,))],
        limit=8,
    )[0]


def attend_kernel(
    row_lengths, cache_lengths, owners, *refs, count, places, sub_rows, heads, tile, divisor
):
    cache, pieces = refs[0], refs[1 : 1 + count]
    q_ref, w_ref, attended_rows, part_ref, held_ref = refs[1 + count : 6 + count]
    w_held, fresh, scores, top, total, acc, sems, w_sems = refs[6 + count :]
    rank = lax.axis_index("dp")
    place = lax.axis_index("tensor")
    row_count = q_ref.shape[0]
    width = part_ref.shape[1]
    docs = row_lengths.shape[1]
    copies = []
    for at, (piece, own) in enumerate(zip(pieces, places)):
        size = piece.shape[0]
        start = 0 if own is None else (rank if own else 1 - rank) * size
        target = fresh.at[pl.ds(pl.multiple_of(start, 16), size)]
        copies.append(pltpu.make_async_copy(piece, target, sems.at[at]))
    w_copies = column_copies(w_ref, (place ^ 3) * width, w_held, w_sems)
    start_copies(copies + w_copies)

    row_start, row_end = documents(row_lengths, docs)
    cache_start, cache_end = documents(cache_lengths, docs)
    stacked = heads * sub_rows
    lanes = 128

    def by_doc(row, values):
        found = values[0]
        for d in range(1, docs):
            found = jnp.where(row >= row_start[d], values[d], found)
        return found

    pairs = jnp.int32(0)
    for block in range(owners.shape[1]):
        found = jnp.int32(0)
        for d in range(docs):
            low = jnp.maximum(row_start[d], block * BLOCK_ROWS)
            high = jnp.maximum(jnp.minimum(row_end[d], (block + 1) * BLOCK_ROWS), low)
            amount = high - low
            found += amount * (cache_lengths[0, d] + 1 - row_start[d])
            found += lax.shift_right_arithmetic((low + high - 1) * amount, 1)
        pairs += jnp.where(owners[0, block] == rank, found, 0)
    held_ref[...] = jnp.full(held_ref.shape, pairs, jnp.int32).astype(jnp.float32) / divisor

    def span(start, end):
        start = lax.div(start, 16) * 16
        return start, lax.div(end - start + tile - 1, tile)

    def tile_start(source, first, t):
        start = first + t * tile
        return start, pl.multiple_of(jnp.minimum(start, source.shape[0] - tile), 16)

    for step in range(row_count // sub_rows):
        spots = slice(step * sub_rows, (step + 1) * sub_rows)
        first_row = rank * row_count + step * sub_rows
        last_row = first_row + sub_rows - 1
        rows = first_row + lax.broadcasted_iota(jnp.int32, (sub_rows, 1), 0)
        queries = jnp.concatenate(
            [q_ref[spots, h * HEAD_SIZE : (h + 1) * HEAD_SIZE] for h in range(heads)], axis=0
        )
        top[...] = jnp.full(top.shape, NEG, jnp.float32)
        total[...] = jnp.zeros(total.shape, jnp.float32)
        acc[...] = jnp.zeros(acc.shape, jnp.float32)

        def score(source, first, base, low, high):
            def body(t, _):
                begin, start = tile_start(source, first, t)
                found = lax.dot_general(
                    queries,
                    source[pl.ds(start, tile), :HEAD_SIZE],
                    (((1,), (1,)), ((), ())),
                    preferred_element_type=jnp.float32,
                )
                spot = start + lax.broadcasted_iota(jnp.int32, (1, tile), 1)
                seen = (spot >= jnp.maximum(low, begin)) & (spot < high)
                found = jnp.where(seen[None], found.reshape(heads, sub_rows, tile), NEG)
                found = found.reshape(stacked, tile)
                scores[base + t] = found
                best = found[:, :lanes]
                for c in range(1, tile // lanes):
                    best = jnp.maximum(best, found[:, c * lanes : (c + 1) * lanes])
                top[...] = jnp.maximum(top[...], best)
                return 0

            return body

        cache_from, cache_tiles = span(by_doc(first_row, cache_start), by_doc(last_row, cache_end))
        new_from, new_tiles = span(by_doc(first_row, row_start), last_row + 1)
        low, high = by_doc(rows, cache_start), by_doc(rows, cache_end)
        lax.fori_loop(0, cache_tiles, score(cache, cache_from, 0, low, high), 0)
        if step == 0:
            wait_copies(copies)
        low, high = by_doc(rows, row_start), rows + 1
        lax.fori_loop(0, new_tiles, score(fresh, new_from, cache_tiles, low, high), 0)
        highest = jnp.max(top[...], axis=1, keepdims=True)

        def weigh(source, first, base):
            def body(t, _):
                _, start = tile_start(source, first, t)
                weights = jnp.exp2((scores[base + t] - highest) * (HEAD_SIZE**-0.5 * LOG2E))
                part = weights[:, :lanes]
                for c in range(1, tile // lanes):
                    part = part + weights[:, c * lanes : (c + 1) * lanes]
                total[...] += part
                acc[...] += jnp.dot(
                    weights.astype(jnp.bfloat16),
                    source[pl.ds(start, tile), HEAD_SIZE:],
                    preferred_element_type=jnp.float32,
                )
                return 0

            return body

        lax.fori_loop(0, cache_tiles, weigh(cache, cache_from, 0), 0)
        lax.fori_loop(0, new_tiles, weigh(fresh, new_from, cache_tiles), 0)
        attended = (acc[...] / jnp.sum(total[...], axis=1, keepdims=True)).astype(jnp.bfloat16)
        for h in range(heads):
            attended_rows[spots, h * HEAD_SIZE : (h + 1) * HEAD_SIZE] = attended[
                h * sub_rows : (h + 1) * sub_rows
            ]
    wait_copies(w_copies)
    part_ref[...] = jnp.dot(
        attended_rows[...], w_held[...], preferred_element_type=jnp.float32
    ).astype(jnp.bfloat16)


def attention(scalars, queries, cache, pieces, places, fresh, w, divisor):
    rows, width = queries.shape
    heads = width // HEAD_SIZE
    tiles = sum(pl.cdiv(amount, KEY_TILE) for amount in (cache.shape[0], fresh))
    sub_rows = BLOCK_ROWS
    while sub_rows > 32 and heads * sub_rows * tiles * KEY_TILE * 4 > SCORE_BYTES:
        sub_rows //= 2
    stacked = heads * sub_rows
    out_width = w.shape[1] // PARTS
    return resident(
        functools.partial(
            attend_kernel,
            count=len(pieces),
            places=places,
            sub_rows=sub_rows,
            heads=heads,
            tile=KEY_TILE,
            divisor=divisor,
        ),
        "attention",
        [((rows, width), jnp.bfloat16), ((rows, out_width), jnp.bfloat16), ((1, 1), jnp.float32)],
        [cache, *pieces, queries],
        scalars,
        weights=[w],
        scratch=[
            pltpu.VMEM((width, out_width), jnp.bfloat16),
            pltpu.VMEM((fresh, 2 * HEAD_SIZE), jnp.bfloat16),
            pltpu.VMEM((tiles, stacked, KEY_TILE), jnp.float32),
            pltpu.VMEM((stacked, 128), jnp.float32),
            pltpu.VMEM((stacked, 128), jnp.float32),
            pltpu.VMEM((stacked, HEAD_SIZE), jnp.float32),
            pltpu.SemaphoreType.DMA((len(pieces),)),
            pltpu.SemaphoreType.DMA((WEIGHT_CUTS,)),
        ],
        limit=26,
        moved=2 * w.size,
    )


def out_kernel(a_ref, w_ref, one, two, same, w_held, sems):
    outs = (one, two, same)
    place = lax.axis_index("tensor")
    spots = (place ^ by_position(place, 1, 2), place ^ by_position(place, 2, 1), place)
    width = same.shape[1]
    copies = [
        column_copies(w_ref, spot * width, w_held.at[at], sems.at[at]) for at, spot in enumerate(spots)
    ]
    for some in copies:
        start_copies(some)
    for at, out_ref in enumerate(outs):
        wait_copies(copies[at])
        out_ref[...] = jnp.dot(
            a_ref[...], w_held[at], preferred_element_type=jnp.float32
        ).astype(jnp.bfloat16)


def out_projection(attended, w):
    rows, depth = attended.shape
    width = w.shape[1] // PARTS
    return resident(
        out_kernel,
        "out_projection",
        [((rows, width), jnp.bfloat16)] * 3,
        [attended],
        weights=[w],
        scratch=[
            pltpu.VMEM((3, depth, width), jnp.bfloat16),
            pltpu.SemaphoreType.DMA((3, WEIGHT_CUTS)),
        ],
        limit=16,
    )


def on_device(
    tokens, norm_gain, w_query, key_value_weight, w_out, cache_kv, cache_lengths, row_lengths, block_owner
):
    ranks = lax.axis_size("dp")
    splits = lax.axis_size("tensor")
    sections = lax.axis_size("pipe")
    rank = lax.axis_index("dp")
    own = tokens[0]
    row_count = own.shape[0]
    cache_rows = cache_kv.shape[1]
    gain, wq, wkv, wo = norm_gain, w_query[0], key_value_weight[0], w_out[0]
    assert splits == PARTS and row_count % BLOCK_ROWS == 0
    inner_pairs = xor_pairs(splits, 3, range(1, splits - 1))
    pair = [(0, 1), (1, 0)] if ranks == 2 else None

    def onwards(block, pairs):
        route = [
            (p * splits + a, (p + 1) % sections * splits + b) for p in range(sections) for a, b in pairs
        ]
        return swap(block, ("pipe", "tensor"), route)

    one = swap(own, "tensor", [(0, 2), (3, 1), (1, 0), (2, 3)])
    square = jnp.sum(jnp.square(own.astype(jnp.float32)), axis=1)[None]
    rest = swap(square, "tensor", xor_pairs(splits, 3))
    one, rest, late = lax.optimization_barrier((one, rest, own))
    two = swap(late, "tensor", [(0, 1), (3, 2), (1, 3), (2, 0)])
    relayed = swap(one, "tensor", [(1, 0), (2, 3)])
    cross = swap(late, "tensor", inner_pairs)
    cache = after(cache_kv.reshape(cache_rows, 2 * HEAD_SIZE), rest)
    if pair:
        other = swap(cache, "dp", pair)
        cache = jnp.where(
            rank == 0, jnp.concatenate([cache, other]), jnp.concatenate([other, cache])
        )
    else:
        cache = lax.all_gather(cache, "dp", axis=0, tiled=True)

    rest = jnp.broadcast_to(rest[0][:, None], (row_count, 128))
    divisor = BLOCK_ROWS * (cache_rows * ranks // 2 + row_count * ranks // 2)
    early_q, early_kv, factor = early_projection(own, one, two, rest, gain, wq, wkv)
    kv, normed = last_kv(cross, relayed, factor, gain, early_kv, wkv)
    if pair:
        pieces, places = [kv, swap(kv, "dp", pair)], (1, 0)
    else:
        pieces, places = [lax.all_gather(kv, "dp", axis=0, tiled=True)], (None,)
    queries = last_q(normed, early_q, wq)
    home = onwards(after(own, kv), xor_pairs(splits, 0))

    scalars = (row_lengths, cache_lengths, block_owner[:, :, 0])
    attended, third, blocks_held = attention(
        scalars, queries, cache, pieces, places, ranks * row_count, wo, float(divisor)
    )
    from_outer = swap(third, "tensor", [(0, 1), (3, 2)])
    from_cross = onwards(third, inner_pairs)
    attended, home = lax.optimization_barrier((attended, home))
    first, second, same = out_projection(attended, wo)
    from_one = onwards(first, [(0, 2), (3, 1), (1, 0), (2, 3)])
    from_same = onwards(same, xor_pairs(splits, 0))
    summed = (second.astype(jnp.float32) + from_outer.astype(jnp.float32)).astype(jnp.bfloat16)
    from_two = onwards(summed, [(0, 1), (3, 2), (1, 3), (2, 0)])
    total = from_same.astype(jnp.float32)
    for block in (from_one, from_two, from_cross):
        total = total + block.astype(jnp.float32)
    handed = (home.astype(jnp.float32) + total).astype(jnp.bfloat16)[None]
    return handed, blocks_held


def solution(mesh):
    placed = (
        P("pipe", "dp", "tensor"),
        P("pipe", None),
        P("pipe", None, "tensor"),
        P("pipe", None, "tensor"),
        P("pipe", "tensor", None),
        P("pipe", "dp", "tensor", None),
        P("pipe", None),
        P("pipe", None),
        P("pipe", None, None),
    )
    return jax.shard_map(
        on_device,
        mesh=mesh,
        in_specs=placed,
        out_specs=(P("pipe", "dp", "tensor"), P("pipe", "dp")),
        check_vma=False,
    )
```

```python
import functools

import jax
import jax.numpy as jnp
from jax import lax
from jax.experimental import pallas as pl
from jax.experimental.pallas import tpu as pltpu
from jax.sharding import PartitionSpec as P

HEAD_SIZE = 128
BLOCK_ROWS = 128
EPS = 1e-06
NEG = -1e30
LOG2E = 1.4426950408889634
MIB = 1024 * 1024
SCORE_BYTES = 13 * MIB
PARTS = 4
WEIGHT_CUTS = 4
CACHE_TILE = 640
NEW_TILE = 512


def swap(block, axis, pairs):
    return lax.ppermute(block, axis, pairs)


def xor_pairs(count, mask, among=None):
    return [(i, i ^ mask) for i in range(count) if among is None or i in among]


def after(value, *others):
    return lax.optimization_barrier((value, *others))[0]


def in_vmem(x):
    return pltpu.with_memory_space_constraint(x, pltpu.VMEM)


def in_hbm(x):
    return pltpu.with_memory_space_constraint(x, pltpu.HBM)


def resident(kernel, name, outs, args, scalars=(), weights=(), scratch=(), limit=16, moved=0):
    spaces = [pl.BlockSpec(memory_space=pltpu.SMEM)] * len(scalars)
    spaces += [pl.BlockSpec(memory_space=pltpu.VMEM)] * len(args)
    spaces += [pl.BlockSpec(memory_space=pl.ANY)] * len(weights)
    return pl.pallas_call(
        kernel,
        in_specs=spaces,
        out_specs=[pl.BlockSpec(memory_space=pltpu.VMEM)] * len(outs),
        out_shape=[
            jax.ShapeDtypeStruct(shape, dtype) if shape == (1, 1) else pltpu.VMEM(shape, dtype)
            for shape, dtype in outs
        ],
        scratch_shapes=list(scratch),
        compiler_params=pltpu.CompilerParams(vmem_limit_bytes=limit * MIB),
        cost_estimate=pl.CostEstimate(flops=0, bytes_accessed=moved, transcendentals=0),
        name=name,
    )(*scalars, *[in_vmem(x) for x in args], *[in_hbm(w) for w in weights])


def start_copies(copies):
    for copy in copies:
        copy.start()


def wait_copies(copies):
    for copy in copies:
        copy.wait()


def row_copies(w_ref, start, held, sems):
    cuts = sems.shape[0]
    rows = held.shape[0] // cuts
    return [
        pltpu.make_async_copy(
            w_ref.at[pl.ds(pl.multiple_of(start + at * rows, 16), rows)],
            held.at[pl.ds(at * rows, rows)],
            sems.at[at],
        )
        for at in range(cuts)
    ]


def column_copies(w_ref, start, held, sems):
    cuts = sems.shape[0]
    rows, width = held.shape
    rows = rows // cuts
    return [
        pltpu.make_async_copy(
            w_ref.at[pl.ds(at * rows, rows), pl.ds(pl.multiple_of(start, 128), width)],
            held.at[pl.ds(at * rows, rows)],
            sems.at[at],
        )
        for at in range(cuts)
    ]


def store_normed(out_ref, x_ref, factor_ref, gain_ref, place):
    width = x_ref.shape[1]
    gain = gain_ref[:, pl.ds(pl.multiple_of(place * width, 128), width)].astype(jnp.float32)
    for c in range(0, width, 128):
        wide = x_ref[:, c : c + 128].astype(jnp.float32)
        out_ref[:, c : c + 128] = (wide * factor_ref[...] * gain[:, c : c + 128]).astype(jnp.bfloat16)


def documents(lengths, docs):
    starts, ends, last = [], [], jnp.int32(0)
    for d in range(docs):
        starts.append(last)
        last = last + lengths[0, d]
        ends.append(last)
    return starts, ends


def by_position(place, for_inner, for_outer):
    return jnp.where((place > 0) & (place < PARTS - 1), for_inner, for_outer)


def early_kernel(
    own, one, two, rest_ref, gain_ref, wq_ref, wkv_ref,
    q_ref, kv_ref, factor_ref, wq_held, wkv_held, normed, sems_q, sems_kv,
):
    place = lax.axis_index("tensor")
    width = own.shape[1]
    shards = (own, one, two)
    spots = (place, place ^ by_position(place, 2, 1), place ^ by_position(place, 1, 2))
    copies = []
    for at in range(len(shards)):
        first, spot = spots[at] * width, pl.ds(at * width, width)
        copies += row_copies(wkv_ref, first, wkv_held.at[spot], sems_kv.at[at])
        copies += row_copies(wq_ref, first, wq_held.at[spot], sems_q.at[at])
    start_copies(copies)
    squares = rest_ref[:, :1]
    for x_ref in shards:
        wide = x_ref[...].astype(jnp.float32)
        squares += jnp.sum(wide * wide, axis=1, keepdims=True)
    factor = lax.rsqrt(squares / (width * (len(shards) + 1)) + EPS)
    factor_ref[...] = jnp.broadcast_to(factor, factor_ref.shape)
    for at, x_ref in enumerate(shards):
        store_normed(normed.at[:, pl.ds(at * width, width)], x_ref, factor_ref, gain_ref, spots[at])
    wait_copies(copies)
    kv_ref[...] = jnp.dot(normed[...], wkv_held[...], preferred_element_type=jnp.float32)
    q_ref[...] = jnp.dot(normed[...], wq_held[...], preferred_element_type=jnp.float32)


def early_projection(own, one, two, rest, gain, wq, wkv):
    rows, width = own.shape
    heads, kv_width = wq.shape[1], wkv.shape[1]
    return resident(
        early_kernel,
        "early_projection",
        [((rows, heads), jnp.float32), ((rows, kv_width), jnp.float32), ((rows, 128), jnp.float32)],
        [own, one, two, rest, gain],
        weights=[wq, wkv],
        scratch=[
            pltpu.VMEM((3 * width, heads), jnp.bfloat16),
            pltpu.VMEM((3 * width, kv_width), jnp.bfloat16),
            pltpu.VMEM((rows, 3 * width), jnp.bfloat16),
            pltpu.SemaphoreType.DMA((3, WEIGHT_CUTS)),
            pltpu.SemaphoreType.DMA((3, 1)),
        ],
        limit=24,
    )


def last_kv_kernel(
    cross, relayed, factor_ref, gain_ref, acc_ref, w_ref, kv_ref, normed, w_held, x, sems
):
    place = lax.axis_index("tensor")
    copies = row_copies(w_ref, (place ^ 3) * x.shape[1], w_held, sems)
    start_copies(copies)
    is_inner = (place > 0) & (place < PARTS - 1)

    @pl.when(is_inner)
    def _():
        store_normed(normed, cross, factor_ref, gain_ref, place ^ 3)

    @pl.when(jnp.logical_not(is_inner))
    def _():
        store_normed(normed, relayed, factor_ref, gain_ref, place ^ 3)

    wait_copies(copies)
    part = jnp.dot(normed[...], w_held[...], preferred_element_type=jnp.float32)
    kv_ref[...] = (acc_ref[...] + part).astype(jnp.bfloat16)


def last_kv(cross, relayed, factor, gain, acc, w):
    rows, columns = acc.shape
    width = relayed.shape[1]
    return resident(
        last_kv_kernel,
        "last_kv",
        [((rows, columns), jnp.bfloat16), ((rows, width), jnp.bfloat16)],
        [cross, relayed, factor, gain, acc],
        weights=[w],
        scratch=[
            pltpu.VMEM((width, columns), jnp.bfloat16),
            pltpu.VMEM((rows, width), jnp.bfloat16),
            pltpu.SemaphoreType.DMA((2,)),
        ],
        limit=8,
    )


def last_q_kernel(normed, acc_ref, w_ref, q_ref, w_held, sems):
    place = lax.axis_index("tensor")
    copies = row_copies(w_ref, (place ^ 3) * normed.shape[1], w_held, sems)
    start_copies(copies)
    wait_copies(copies)
    part = jnp.dot(normed[...], w_held[...], preferred_element_type=jnp.float32)
    q_ref[...] = (acc_ref[...] + part).astype(jnp.bfloat16)


def last_q(normed, acc, w):
    rows, width = normed.shape
    columns = w.shape[1]
    return resident(
        last_q_kernel,
        "last_q",
        [((rows, columns), jnp.bfloat16)],
        [normed, acc],
        weights=[w],
        scratch=[pltpu.VMEM((width, columns), jnp.bfloat16), pltpu.SemaphoreType.DMA((WEIGHT_CUTS,))],
        limit=8,
    )[0]


def attend_kernel(
    row_lengths, cache_lengths, owners, *refs, count, places, sub_rows, heads, divisor
):
    cache, pieces = refs[0], refs[1 : 1 + count]
    q_ref, w_ref, attended_rows, part_ref, held_ref = refs[1 + count : 6 + count]
    w_held, fresh, old_scores, new_scores, top, total, acc, sems, w_sems = refs[6 + count :]
    rank = lax.axis_index("dp")
    place = lax.axis_index("tensor")
    row_count = q_ref.shape[0]
    width = part_ref.shape[1]
    docs = row_lengths.shape[1]
    copies = []
    for at, (piece, own) in enumerate(zip(pieces, places)):
        size = piece.shape[0]
        start = 0 if own is None else (rank if own else 1 - rank) * size
        target = fresh.at[pl.ds(pl.multiple_of(start, 16), size)]
        copies.append(pltpu.make_async_copy(piece, target, sems.at[at]))
    w_copies = column_copies(w_ref, (place ^ 3) * width, w_held, w_sems)
    start_copies(copies + w_copies)

    row_start, row_end = documents(row_lengths, docs)
    cache_start, cache_end = documents(cache_lengths, docs)
    stacked = heads * sub_rows
    lanes = 128

    def by_doc(row, values):
        found = values[0]
        for d in range(1, docs):
            found = jnp.where(row >= row_start[d], values[d], found)
        return found

    pairs = jnp.int32(0)
    for block in range(owners.shape[1]):
        found = jnp.int32(0)
        for d in range(docs):
            low = jnp.maximum(row_start[d], block * BLOCK_ROWS)
            high = jnp.maximum(jnp.minimum(row_end[d], (block + 1) * BLOCK_ROWS), low)
            amount = high - low
            found += amount * (cache_lengths[0, d] + 1 - row_start[d])
            found += lax.shift_right_arithmetic((low + high - 1) * amount, 1)
        pairs += jnp.where(owners[0, block] == rank, found, 0)
    held_ref[...] = jnp.full(held_ref.shape, pairs, jnp.int32).astype(jnp.float32) / divisor

    def span(scores, start, end):
        tile = scores.shape[2]
        start = lax.div(start, 16) * 16
        return start, lax.div(end - start + tile - 1, tile)

    def tile_start(scores, source, first, t):
        tile = scores.shape[2]
        start = first + t * tile
        return start, pl.multiple_of(jnp.minimum(start, source.shape[0] - tile), 16)

    def lane_blocks(values):
        return [values[:, c : c + lanes] for c in range(0, values.shape[1], lanes)]

    for step in range(row_count // sub_rows):
        spots = slice(step * sub_rows, (step + 1) * sub_rows)
        first_row = rank * row_count + step * sub_rows
        last_row = first_row + sub_rows - 1
        rows = first_row + lax.broadcasted_iota(jnp.int32, (sub_rows, 1), 0)
        queries = jnp.concatenate(
            [q_ref[spots, h * HEAD_SIZE : (h + 1) * HEAD_SIZE] for h in range(heads)], axis=0
        )
        top[...] = jnp.full(top.shape, NEG, jnp.float32)
        total[...] = jnp.zeros(total.shape, jnp.float32)
        acc[...] = jnp.zeros(acc.shape, jnp.float32)

        def score(scores, source, first, low, high):
            tile = scores.shape[2]

            def body(t, _):
                begin, start = tile_start(scores, source, first, t)
                found = lax.dot_general(
                    queries,
                    source[pl.ds(start, tile), :HEAD_SIZE],
                    (((1,), (1,)), ((), ())),
                    preferred_element_type=jnp.float32,
                )
                spot = start + lax.broadcasted_iota(jnp.int32, (1, tile), 1)
                seen = (spot >= jnp.maximum(low, begin)) & (spot < high)
                found = jnp.where(seen[None], found.reshape(heads, sub_rows, tile), NEG)
                found = found.reshape(stacked, tile)
                scores[t] = found
                top[...] = functools.reduce(jnp.maximum, lane_blocks(found), top[...])
                return 0

            return body

        cache_from, cache_tiles = span(
            old_scores, by_doc(first_row, cache_start), by_doc(last_row, cache_end)
        )
        new_from, new_tiles = span(new_scores, by_doc(first_row, row_start), last_row + 1)
        low, high = by_doc(rows, cache_start), by_doc(rows, cache_end)
        lax.fori_loop(0, cache_tiles, score(old_scores, cache, cache_from, low, high), 0)
        if step == 0:
            wait_copies(copies)
        low, high = by_doc(rows, row_start), rows + 1
        lax.fori_loop(0, new_tiles, score(new_scores, fresh, new_from, low, high), 0)
        top[...] = jnp.broadcast_to(jnp.max(top[...], axis=1, keepdims=True), top.shape)

        def weigh(scores, source, first):
            tile = scores.shape[2]

            def body(t, _):
                _, start = tile_start(scores, source, first, t)
                highest = top[...]
                weights = [
                    jnp.exp2((scores[t, :, c : c + lanes] - highest) * (HEAD_SIZE**-0.5 * LOG2E))
                    for c in range(0, tile, lanes)
                ]
                total[...] = functools.reduce(jnp.add, weights, total[...])
                acc[...] += jnp.dot(
                    jnp.concatenate([w.astype(jnp.bfloat16) for w in weights], axis=1),
                    source[pl.ds(start, tile), HEAD_SIZE:],
                    preferred_element_type=jnp.float32,
                )
                return 0

            return body

        lax.fori_loop(0, cache_tiles, weigh(old_scores, cache, cache_from), 0)
        lax.fori_loop(0, new_tiles, weigh(new_scores, fresh, new_from), 0)
        attended = (acc[...] / jnp.sum(total[...], axis=1, keepdims=True)).astype(jnp.bfloat16)
        for h in range(heads):
            attended_rows[spots, h * HEAD_SIZE : (h + 1) * HEAD_SIZE] = attended[
                h * sub_rows : (h + 1) * sub_rows
            ]
    wait_copies(w_copies)
    part_ref[...] = jnp.dot(
        attended_rows[...], w_held[...], preferred_element_type=jnp.float32
    ).astype(jnp.bfloat16)


def attention(scalars, queries, cache, pieces, places, fresh, w, divisor):
    rows, width = queries.shape
    heads = width // HEAD_SIZE
    sizes = [(pl.cdiv(cache.shape[0], CACHE_TILE), CACHE_TILE), (pl.cdiv(fresh, NEW_TILE), NEW_TILE)]
    sub_rows = BLOCK_ROWS
    while sub_rows > 32 and heads * sub_rows * 4 * sum(a * b for a, b in sizes) > SCORE_BYTES:
        sub_rows //= 2
    stacked = heads * sub_rows
    out_width = w.shape[1] // PARTS
    return resident(
        functools.partial(
            attend_kernel,
            count=len(pieces),
            places=places,
            sub_rows=sub_rows,
            heads=heads,
            divisor=divisor,
        ),
        "attention",
        [((rows, width), jnp.bfloat16), ((rows, out_width), jnp.bfloat16), ((1, 1), jnp.float32)],
        [cache, *pieces, queries],
        scalars,
        weights=[w],
        scratch=[
            pltpu.VMEM((width, out_width), jnp.bfloat16),
            pltpu.VMEM((fresh, 2 * HEAD_SIZE), jnp.bfloat16),
            *(pltpu.VMEM((tiles, stacked, tile), jnp.float32) for tiles, tile in sizes),
            pltpu.VMEM((stacked, 128), jnp.float32),
            pltpu.VMEM((stacked, 128), jnp.float32),
            pltpu.VMEM((stacked, HEAD_SIZE), jnp.float32),
            pltpu.SemaphoreType.DMA((len(pieces),)),
            pltpu.SemaphoreType.DMA((WEIGHT_CUTS,)),
        ],
        limit=26,
        moved=2 * w.size,
    )


def out_kernel(a_ref, w_ref, one, two, same, w_held, sems):
    outs = (one, two, same)
    place = lax.axis_index("tensor")
    spots = (place ^ by_position(place, 1, 2), place ^ by_position(place, 2, 1), place)
    width = same.shape[1]
    copies = [
        column_copies(w_ref, spot * width, w_held.at[at], sems.at[at]) for at, spot in enumerate(spots)
    ]
    for some in copies:
        start_copies(some)
    for at, out_ref in enumerate(outs):
        wait_copies(copies[at])
        out_ref[...] = jnp.dot(
            a_ref[...], w_held[at], preferred_element_type=jnp.float32
        ).astype(jnp.bfloat16)


def out_projection(attended, w):
    rows, depth = attended.shape
    width = w.shape[1] // PARTS
    return resident(
        out_kernel,
        "out_projection",
        [((rows, width), jnp.bfloat16)] * 3,
        [attended],
        weights=[w],
        scratch=[
            pltpu.VMEM((3, depth, width), jnp.bfloat16),
            pltpu.SemaphoreType.DMA((3, WEIGHT_CUTS)),
        ],
        limit=16,
    )


def on_device(
    tokens, norm_gain, w_query, key_value_weight, w_out, cache_kv, cache_lengths, row_lengths, block_owner
):
    ranks = lax.axis_size("dp")
    splits = lax.axis_size("tensor")
    sections = lax.axis_size("pipe")
    rank = lax.axis_index("dp")
    own = tokens[0]
    row_count = own.shape[0]
    cache_rows = cache_kv.shape[1]
    gain, wq, wkv, wo = norm_gain, w_query[0], key_value_weight[0], w_out[0]
    assert splits == PARTS and row_count % BLOCK_ROWS == 0
    inner_pairs = xor_pairs(splits, 3, range(1, splits - 1))
    pair = [(0, 1), (1, 0)] if ranks == 2 else None

    def onwards(block, pairs):
        route = [
            (p * splits + a, (p + 1) % sections * splits + b) for p in range(sections) for a, b in pairs
        ]
        return swap(block, ("pipe", "tensor"), route)

    one = swap(own, "tensor", [(0, 2), (3, 1), (1, 0), (2, 3)])
    square = jnp.sum(jnp.square(own.astype(jnp.float32)), axis=1)[None]
    rest = swap(square, "tensor", xor_pairs(splits, 3))
    one, rest, late = lax.optimization_barrier((one, rest, own))
    two = swap(late, "tensor", [(0, 1), (3, 2), (1, 3), (2, 0)])
    relayed = swap(one, "tensor", [(1, 0), (2, 3)])
    cross = swap(late, "tensor", inner_pairs)
    cache = after(cache_kv.reshape(cache_rows, 2 * HEAD_SIZE), rest)
    if pair:
        other = swap(cache, "dp", pair)
        cache = jnp.where(
            rank == 0, jnp.concatenate([cache, other]), jnp.concatenate([other, cache])
        )
    else:
        cache = lax.all_gather(cache, "dp", axis=0, tiled=True)

    rest = jnp.broadcast_to(rest[0][:, None], (row_count, 128))
    divisor = BLOCK_ROWS * (cache_rows * ranks // 2 + row_count * ranks // 2)
    early_q, early_kv, factor = early_projection(own, one, two, rest, gain, wq, wkv)
    kv, normed = last_kv(cross, relayed, factor, gain, early_kv, wkv)
    if pair:
        pieces, places = [kv, swap(kv, "dp", pair)], (1, 0)
    else:
        pieces, places = [lax.all_gather(kv, "dp", axis=0, tiled=True)], (None,)
    queries = last_q(normed, early_q, wq)
    home = onwards(after(own, kv), xor_pairs(splits, 0))

    scalars = (row_lengths, cache_lengths, block_owner[:, :, 0])
    attended, third, blocks_held = attention(
        scalars, queries, cache, pieces, places, ranks * row_count, wo, float(divisor)
    )
    from_outer = swap(third, "tensor", [(0, 1), (3, 2)])
    from_cross = onwards(third, inner_pairs)
    attended, home = lax.optimization_barrier((attended, home))
    first, second, same = out_projection(attended, wo)
    from_one = onwards(first, [(0, 2), (3, 1), (1, 0), (2, 3)])
    from_same = onwards(same, xor_pairs(splits, 0))
    summed = (second.astype(jnp.float32) + from_outer.astype(jnp.float32)).astype(jnp.bfloat16)
    from_two = onwards(summed, [(0, 1), (3, 2), (1, 3), (2, 0)])
    total = from_same.astype(jnp.float32)
    for block in (from_one, from_two, from_cross):
        total = total + block.astype(jnp.float32)
    handed = (home.astype(jnp.float32) + total).astype(jnp.bfloat16)[None]
    return handed, blocks_held


def solution(mesh):
    placed = (
        P("pipe", "dp", "tensor"),
        P("pipe", None),
        P("pipe", None, "tensor"),
        P("pipe", None, "tensor"),
        P("pipe", "tensor", None),
        P("pipe", "dp", "tensor", None),
        P("pipe", None),
        P("pipe", None),
        P("pipe", None, None),
    )
    return jax.shard_map(
        on_device,
        mesh=mesh,
        in_specs=placed,
        out_specs=(P("pipe", "dp", "tensor"), P("pipe", "dp")),
        check_vma=False,
    )
```

```python
import functools

import jax
import jax.numpy as jnp
from jax import lax
from jax.experimental import pallas as pl
from jax.experimental.pallas import tpu as pltpu
from jax.sharding import PartitionSpec as P

HEAD_SIZE = 128
BLOCK_ROWS = 128
EPS = 1e-06
NEG = -1e30
LOG2E = 1.4426950408889634
MIB = 1024 * 1024
SCORE_BYTES = 13 * MIB
PARTS = 4
WEIGHT_CUTS = 4
CACHE_TILE = 768
NEW_TILE = 512


def swap(block, axis, pairs):
    return lax.ppermute(block, axis, pairs)


def xor_pairs(count, mask, among=None):
    return [(i, i ^ mask) for i in range(count) if among is None or i in among]


def after(value, *others):
    return lax.optimization_barrier((value, *others))[0]


def in_vmem(x):
    return pltpu.with_memory_space_constraint(x, pltpu.VMEM)


def in_hbm(x):
    return pltpu.with_memory_space_constraint(x, pltpu.HBM)


def resident(kernel, name, outs, args, scalars=(), weights=(), scratch=(), limit=16, moved=0):
    spaces = [pl.BlockSpec(memory_space=pltpu.SMEM)] * len(scalars)
    spaces += [pl.BlockSpec(memory_space=pltpu.VMEM)] * len(args)
    spaces += [pl.BlockSpec(memory_space=pl.ANY)] * len(weights)
    return pl.pallas_call(
        kernel,
        in_specs=spaces,
        out_specs=[pl.BlockSpec(memory_space=pltpu.VMEM)] * len(outs),
        out_shape=[
            jax.ShapeDtypeStruct(shape, dtype) if shape == (1, 1) else pltpu.VMEM(shape, dtype)
            for shape, dtype in outs
        ],
        scratch_shapes=list(scratch),
        compiler_params=pltpu.CompilerParams(vmem_limit_bytes=limit * MIB),
        cost_estimate=pl.CostEstimate(flops=0, bytes_accessed=moved, transcendentals=0),
        name=name,
    )(*scalars, *[in_vmem(x) for x in args], *[in_hbm(w) for w in weights])


def start_copies(copies):
    for copy in copies:
        copy.start()


def wait_copies(copies):
    for copy in copies:
        copy.wait()


def row_copies(w_ref, start, held, sems):
    cuts = sems.shape[0]
    rows = held.shape[0] // cuts
    return [
        pltpu.make_async_copy(
            w_ref.at[pl.ds(pl.multiple_of(start + at * rows, 16), rows)],
            held.at[pl.ds(at * rows, rows)],
            sems.at[at],
        )
        for at in range(cuts)
    ]


def column_copies(w_ref, start, held, sems):
    cuts = sems.shape[0]
    rows, width = held.shape
    rows = rows // cuts
    return [
        pltpu.make_async_copy(
            w_ref.at[pl.ds(at * rows, rows), pl.ds(pl.multiple_of(start, 128), width)],
            held.at[pl.ds(at * rows, rows)],
            sems.at[at],
        )
        for at in range(cuts)
    ]


def store_normed(out_ref, x_ref, factor_ref, gain_ref, place):
    width = x_ref.shape[1]
    gain = gain_ref[:, pl.ds(pl.multiple_of(place * width, 128), width)].astype(jnp.float32)
    for c in range(0, width, 128):
        wide = x_ref[:, c : c + 128].astype(jnp.float32)
        out_ref[:, c : c + 128] = (wide * factor_ref[...] * gain[:, c : c + 128]).astype(jnp.bfloat16)


def documents(lengths, docs):
    starts, ends, last = [], [], jnp.int32(0)
    for d in range(docs):
        starts.append(last)
        last = last + lengths[0, d]
        ends.append(last)
    return starts, ends


def by_position(place, for_inner, for_outer):
    return jnp.where((place > 0) & (place < PARTS - 1), for_inner, for_outer)


def early_kernel(
    own, one, two, rest_ref, gain_ref, wq_ref, wkv_ref,
    q_ref, kv_ref, factor_ref, wq_held, wkv_held, normed, sems_q, sems_kv,
):
    place = lax.axis_index("tensor")
    width = own.shape[1]
    shards = (own, one, two)
    spots = (place, place ^ by_position(place, 2, 1), place ^ by_position(place, 1, 2))
    copies = []
    for at in range(len(shards)):
        first, spot = spots[at] * width, pl.ds(at * width, width)
        copies += row_copies(wkv_ref, first, wkv_held.at[spot], sems_kv.at[at])
        copies += row_copies(wq_ref, first, wq_held.at[spot], sems_q.at[at])
    start_copies(copies)
    squares = rest_ref[:, :1]
    for x_ref in shards:
        wide = x_ref[...].astype(jnp.float32)
        squares += jnp.sum(wide * wide, axis=1, keepdims=True)
    factor = lax.rsqrt(squares / (width * (len(shards) + 1)) + EPS)
    factor_ref[...] = jnp.broadcast_to(factor, factor_ref.shape)
    for at, x_ref in enumerate(shards):
        store_normed(normed.at[:, pl.ds(at * width, width)], x_ref, factor_ref, gain_ref, spots[at])
    wait_copies(copies)
    kv_ref[...] = jnp.dot(normed[...], wkv_held[...], preferred_element_type=jnp.float32)
    q_ref[...] = jnp.dot(normed[...], wq_held[...], preferred_element_type=jnp.float32)


def early_projection(own, one, two, rest, gain, wq, wkv):
    rows, width = own.shape
    heads, kv_width = wq.shape[1], wkv.shape[1]
    return resident(
        early_kernel,
        "early_projection",
        [((rows, heads), jnp.float32), ((rows, kv_width), jnp.float32), ((rows, 128), jnp.float32)],
        [own, one, two, rest, gain],
        weights=[wq, wkv],
        scratch=[
            pltpu.VMEM((3 * width, heads), jnp.bfloat16),
            pltpu.VMEM((3 * width, kv_width), jnp.bfloat16),
            pltpu.VMEM((rows, 3 * width), jnp.bfloat16),
            pltpu.SemaphoreType.DMA((3, WEIGHT_CUTS)),
            pltpu.SemaphoreType.DMA((3, 1)),
        ],
        limit=24,
    )


def last_kv_kernel(
    cross, relayed, factor_ref, gain_ref, acc_ref, w_ref, kv_ref, normed, w_held, x, sems
):
    place = lax.axis_index("tensor")
    copies = row_copies(w_ref, (place ^ 3) * x.shape[1], w_held, sems)
    start_copies(copies)
    is_inner = (place > 0) & (place < PARTS - 1)

    @pl.when(is_inner)
    def _():
        store_normed(normed, cross, factor_ref, gain_ref, place ^ 3)

    @pl.when(jnp.logical_not(is_inner))
    def _():
        store_normed(normed, relayed, factor_ref, gain_ref, place ^ 3)

    wait_copies(copies)
    part = jnp.dot(normed[...], w_held[...], preferred_element_type=jnp.float32)
    kv_ref[...] = (acc_ref[...] + part).astype(jnp.bfloat16)


def last_kv(cross, relayed, factor, gain, acc, w):
    rows, columns = acc.shape
    width = relayed.shape[1]
    return resident(
        last_kv_kernel,
        "last_kv",
        [((rows, columns), jnp.bfloat16), ((rows, width), jnp.bfloat16)],
        [cross, relayed, factor, gain, acc],
        weights=[w],
        scratch=[
            pltpu.VMEM((width, columns), jnp.bfloat16),
            pltpu.VMEM((rows, width), jnp.bfloat16),
            pltpu.SemaphoreType.DMA((2,)),
        ],
        limit=8,
    )


def last_q_kernel(normed, acc_ref, w_ref, q_ref, w_held, sems):
    place = lax.axis_index("tensor")
    copies = row_copies(w_ref, (place ^ 3) * normed.shape[1], w_held, sems)
    start_copies(copies)
    wait_copies(copies)
    part = jnp.dot(normed[...], w_held[...], preferred_element_type=jnp.float32)
    q_ref[...] = (acc_ref[...] + part).astype(jnp.bfloat16)


def last_q(normed, acc, w):
    rows, width = normed.shape
    columns = w.shape[1]
    return resident(
        last_q_kernel,
        "last_q",
        [((rows, columns), jnp.bfloat16)],
        [normed, acc],
        weights=[w],
        scratch=[pltpu.VMEM((width, columns), jnp.bfloat16), pltpu.SemaphoreType.DMA((WEIGHT_CUTS,))],
        limit=8,
    )[0]


def attend_kernel(
    row_lengths, cache_lengths, owners, *refs, count, places, sub_rows, heads, divisor
):
    cache, pieces = refs[0], refs[1 : 1 + count]
    q_ref, w_ref, attended_rows, part_ref, held_ref = refs[1 + count : 6 + count]
    w_held, fresh, old_scores, new_scores, top, total, acc, sems, w_sems = refs[6 + count :]
    rank = lax.axis_index("dp")
    place = lax.axis_index("tensor")
    row_count = q_ref.shape[0]
    width = part_ref.shape[1]
    docs = row_lengths.shape[1]
    copies = []
    for at, (piece, own) in enumerate(zip(pieces, places)):
        size = piece.shape[0]
        start = 0 if own is None else (rank if own else 1 - rank) * size
        target = fresh.at[pl.ds(pl.multiple_of(start, 16), size)]
        copies.append(pltpu.make_async_copy(piece, target, sems.at[at]))
    w_copies = column_copies(w_ref, (place ^ 3) * width, w_held, w_sems)
    start_copies(copies + w_copies)

    row_start, row_end = documents(row_lengths, docs)
    cache_start, cache_end = documents(cache_lengths, docs)
    stacked = heads * sub_rows
    lanes = 128

    def by_doc(row, values):
        found = values[0]
        for d in range(1, docs):
            found = jnp.where(row >= row_start[d], values[d], found)
        return found

    pairs = jnp.int32(0)
    for block in range(owners.shape[1]):
        found = jnp.int32(0)
        for d in range(docs):
            low = jnp.maximum(row_start[d], block * BLOCK_ROWS)
            high = jnp.maximum(jnp.minimum(row_end[d], (block + 1) * BLOCK_ROWS), low)
            amount = high - low
            found += amount * (cache_lengths[0, d] + 1 - row_start[d])
            found += lax.shift_right_arithmetic((low + high - 1) * amount, 1)
        pairs += jnp.where(owners[0, block] == rank, found, 0)
    held_ref[...] = jnp.full(held_ref.shape, pairs, jnp.int32).astype(jnp.float32) / divisor

    def span(scores, start, end):
        tile = scores.shape[2]
        start = lax.div(start, 16) * 16
        return start, lax.div(end - start + tile - 1, tile)

    def tile_start(scores, source, first, t):
        tile = scores.shape[2]
        start = first + t * tile
        return start, pl.multiple_of(jnp.minimum(start, source.shape[0] - tile), 16)

    def lane_blocks(values):
        return [values[:, c : c + lanes] for c in range(0, values.shape[1], lanes)]

    for step in range(row_count // sub_rows):
        spots = slice(step * sub_rows, (step + 1) * sub_rows)
        first_row = rank * row_count + step * sub_rows
        last_row = first_row + sub_rows - 1
        rows = first_row + lax.broadcasted_iota(jnp.int32, (sub_rows, 1), 0)
        queries = jnp.concatenate(
            [q_ref[spots, h * HEAD_SIZE : (h + 1) * HEAD_SIZE] for h in range(heads)], axis=0
        )
        top[...] = jnp.full(top.shape, NEG, jnp.float32)
        total[...] = jnp.zeros(total.shape, jnp.float32)
        acc[...] = jnp.zeros(acc.shape, jnp.float32)

        def score(scores, source, first, low, high):
            tile = scores.shape[2]

            def body(t, _):
                begin, start = tile_start(scores, source, first, t)
                found = lax.dot_general(
                    queries,
                    source[pl.ds(start, tile), :HEAD_SIZE],
                    (((1,), (1,)), ((), ())),
                    preferred_element_type=jnp.float32,
                )
                spot = start + lax.broadcasted_iota(jnp.int32, (1, tile), 1)
                seen = (spot >= jnp.maximum(low, begin)) & (spot < high)
                found = jnp.where(seen[None], found.reshape(heads, sub_rows, tile), NEG)
                found = found.reshape(stacked, tile)
                scores[t] = found
                top[...] = functools.reduce(jnp.maximum, lane_blocks(found), top[...])
                return 0

            return body

        cache_from, cache_tiles = span(
            old_scores, by_doc(first_row, cache_start), by_doc(last_row, cache_end)
        )
        new_from, new_tiles = span(new_scores, by_doc(first_row, row_start), last_row + 1)
        low, high = by_doc(rows, cache_start), by_doc(rows, cache_end)
        lax.fori_loop(0, cache_tiles, score(old_scores, cache, cache_from, low, high), 0)
        if step == 0:
            wait_copies(copies)
        low, high = by_doc(rows, row_start), rows + 1
        lax.fori_loop(0, new_tiles, score(new_scores, fresh, new_from, low, high), 0)
        top[...] = jnp.broadcast_to(jnp.max(top[...], axis=1, keepdims=True), top.shape)

        def weigh(scores, source, first):
            tile = scores.shape[2]

            def body(t, _):
                _, start = tile_start(scores, source, first, t)
                highest = top[...]
                weights = [
                    jnp.exp2((scores[t, :, c : c + lanes] - highest) * (HEAD_SIZE**-0.5 * LOG2E))
                    for c in range(0, tile, lanes)
                ]
                total[...] = functools.reduce(jnp.add, weights, total[...])
                acc[...] += jnp.dot(
                    jnp.concatenate([w.astype(jnp.bfloat16) for w in weights], axis=1),
                    source[pl.ds(start, tile), HEAD_SIZE:],
                    preferred_element_type=jnp.float32,
                )
                return 0

            return body

        lax.fori_loop(0, cache_tiles, weigh(old_scores, cache, cache_from), 0)
        lax.fori_loop(0, new_tiles, weigh(new_scores, fresh, new_from), 0)
        attended = (acc[...] / jnp.sum(total[...], axis=1, keepdims=True)).astype(jnp.bfloat16)
        for h in range(heads):
            attended_rows[spots, h * HEAD_SIZE : (h + 1) * HEAD_SIZE] = attended[
                h * sub_rows : (h + 1) * sub_rows
            ]
    wait_copies(w_copies)
    part_ref[...] = jnp.dot(
        attended_rows[...], w_held[...], preferred_element_type=jnp.float32
    ).astype(jnp.bfloat16)


def attention(scalars, queries, cache, pieces, places, fresh, w, divisor):
    rows, width = queries.shape
    heads = width // HEAD_SIZE
    sizes = [(pl.cdiv(cache.shape[0], CACHE_TILE), CACHE_TILE), (pl.cdiv(fresh, NEW_TILE), NEW_TILE)]
    sub_rows = BLOCK_ROWS
    while sub_rows > 32 and heads * sub_rows * 4 * sum(a * b for a, b in sizes) > SCORE_BYTES:
        sub_rows //= 2
    stacked = heads * sub_rows
    out_width = w.shape[1] // PARTS
    return resident(
        functools.partial(
            attend_kernel,
            count=len(pieces),
            places=places,
            sub_rows=sub_rows,
            heads=heads,
            divisor=divisor,
        ),
        "attention",
        [((rows, width), jnp.bfloat16), ((rows, out_width), jnp.bfloat16), ((1, 1), jnp.float32)],
        [cache, *pieces, queries],
        scalars,
        weights=[w],
        scratch=[
            pltpu.VMEM((width, out_width), jnp.bfloat16),
            pltpu.VMEM((fresh, 2 * HEAD_SIZE), jnp.bfloat16),
            *(pltpu.VMEM((tiles, stacked, tile), jnp.float32) for tiles, tile in sizes),
            pltpu.VMEM((stacked, 128), jnp.float32),
            pltpu.VMEM((stacked, 128), jnp.float32),
            pltpu.VMEM((stacked, HEAD_SIZE), jnp.float32),
            pltpu.SemaphoreType.DMA((len(pieces),)),
            pltpu.SemaphoreType.DMA((WEIGHT_CUTS,)),
        ],
        limit=26,
        moved=2 * w.size,
    )


def out_kernel(a_ref, w_ref, one, two, same, w_held, sems):
    outs = (one, two, same)
    place = lax.axis_index("tensor")
    spots = (place ^ by_position(place, 1, 2), place ^ by_position(place, 2, 1), place)
    width = same.shape[1]
    copies = [
        column_copies(w_ref, spot * width, w_held.at[at], sems.at[at]) for at, spot in enumerate(spots)
    ]
    for some in copies:
        start_copies(some)
    for at, out_ref in enumerate(outs):
        wait_copies(copies[at])
        out_ref[...] = jnp.dot(
            a_ref[...], w_held[at], preferred_element_type=jnp.float32
        ).astype(jnp.bfloat16)


def out_projection(attended, w):
    rows, depth = attended.shape
    width = w.shape[1] // PARTS
    return resident(
        out_kernel,
        "out_projection",
        [((rows, width), jnp.bfloat16)] * 3,
        [attended],
        weights=[w],
        scratch=[
            pltpu.VMEM((3, depth, width), jnp.bfloat16),
            pltpu.SemaphoreType.DMA((3, WEIGHT_CUTS)),
        ],
        limit=16,
    )


def on_device(
    tokens, norm_gain, w_query, key_value_weight, w_out, cache_kv, cache_lengths, row_lengths, block_owner
):
    ranks = lax.axis_size("dp")
    splits = lax.axis_size("tensor")
    sections = lax.axis_size("pipe")
    rank = lax.axis_index("dp")
    own = tokens[0]
    row_count = own.shape[0]
    cache_rows = cache_kv.shape[1]
    gain, wq, wkv, wo = norm_gain, w_query[0], key_value_weight[0], w_out[0]
    assert splits == PARTS and row_count % BLOCK_ROWS == 0
    inner_pairs = xor_pairs(splits, 3, range(1, splits - 1))
    pair = [(0, 1), (1, 0)] if ranks == 2 else None

    def onwards(block, pairs):
        route = [
            (p * splits + a, (p + 1) % sections * splits + b) for p in range(sections) for a, b in pairs
        ]
        return swap(block, ("pipe", "tensor"), route)

    one = swap(own, "tensor", [(0, 2), (3, 1), (1, 0), (2, 3)])
    square = jnp.sum(jnp.square(own.astype(jnp.float32)), axis=1)[None]
    rest = swap(square, "tensor", xor_pairs(splits, 3))
    one, rest, late = lax.optimization_barrier((one, rest, own))
    two = swap(late, "tensor", [(0, 1), (3, 2), (1, 3), (2, 0)])
    cross = swap(late, "tensor", inner_pairs)
    relayed = swap(one, "tensor", [(1, 0), (2, 3)])
    cache = after(cache_kv.reshape(cache_rows, 2 * HEAD_SIZE), rest)
    if pair:
        other = swap(cache, "dp", pair)
        cache = jnp.where(
            rank == 0, jnp.concatenate([cache, other]), jnp.concatenate([other, cache])
        )
    else:
        cache = lax.all_gather(cache, "dp", axis=0, tiled=True)

    rest = jnp.broadcast_to(rest[0][:, None], (row_count, 128))
    divisor = BLOCK_ROWS * (cache_rows * ranks // 2 + row_count * ranks // 2)
    early_q, early_kv, factor = early_projection(own, one, two, rest, gain, wq, wkv)
    kv, normed = last_kv(cross, relayed, factor, gain, early_kv, wkv)
    if pair:
        pieces, places = [kv, swap(kv, "dp", pair)], (1, 0)
    else:
        pieces, places = [lax.all_gather(kv, "dp", axis=0, tiled=True)], (None,)
    queries = last_q(normed, early_q, wq)
    home = onwards(after(own, kv), xor_pairs(splits, 0))

    scalars = (row_lengths, cache_lengths, block_owner[:, :, 0])
    attended, third, blocks_held = attention(
        scalars, queries, cache, pieces, places, ranks * row_count, wo, float(divisor)
    )
    from_outer = swap(third, "tensor", [(0, 1), (3, 2)])
    from_cross = onwards(third, inner_pairs)
    attended, home = lax.optimization_barrier((attended, home))
    from_cross, from_outer = lax.optimization_barrier((from_cross, from_outer))
    first, second, same = out_projection(attended, wo)
    from_one = onwards(first, [(0, 2), (3, 1), (1, 0), (2, 3)])
    summed = (second.astype(jnp.float32) + from_outer.astype(jnp.float32)).astype(jnp.bfloat16)
    from_two = onwards(summed, [(0, 1), (3, 2), (1, 3), (2, 0)])
    from_one, same = lax.optimization_barrier((from_one, same))
    from_same = onwards(same, xor_pairs(splits, 0))
    total = from_same.astype(jnp.float32)
    for block in (from_one, from_two, from_cross):
        total = total + block.astype(jnp.float32)
    handed = (home.astype(jnp.float32) + total).astype(jnp.bfloat16)[None]
    return handed, blocks_held


def solution(mesh):
    placed = (
        P("pipe", "dp", "tensor"),
        P("pipe", None),
        P("pipe", None, "tensor"),
        P("pipe", None, "tensor"),
        P("pipe", "tensor", None),
        P("pipe", "dp", "tensor", None),
        P("pipe", None),
        P("pipe", None),
        P("pipe", None, None),
    )
    return jax.shard_map(
        on_device,
        mesh=mesh,
        in_specs=placed,
        out_specs=(P("pipe", "dp", "tensor"), P("pipe", "dp")),
        check_vma=False,
    )
```

```python
import functools

import jax
import jax.numpy as jnp
from jax import lax
from jax.experimental import pallas as pl
from jax.experimental.pallas import tpu as pltpu
from jax.sharding import PartitionSpec as P

HEAD_SIZE = 128
BLOCK_ROWS = 128
EPS = 1e-06
NEG = -1e30
LOG2E = 1.4426950408889634
MIB = 1024 * 1024
SCORE_BYTES = 13 * MIB
PARTS = 4
WEIGHT_CUTS = 4
CACHE_TILE = 768
NEW_TILE = 512


def swap(block, axis, pairs):
    return lax.ppermute(block, axis, pairs)


def xor_pairs(count, mask, among=None):
    return [(i, i ^ mask) for i in range(count) if among is None or i in among]


def after(value, *others):
    return lax.optimization_barrier((value, *others))[0]


def in_hbm(x):
    return pltpu.with_memory_space_constraint(x, pltpu.HBM)


def resident(kernel, name, outs, args, scalars=(), weights=(), scratch=(), limit=16, moved=0):
    spaces = [pl.BlockSpec(memory_space=pltpu.SMEM)] * len(scalars)
    spaces += [pl.BlockSpec(memory_space=pltpu.VMEM)] * len(args)
    spaces += [pl.BlockSpec(memory_space=pl.ANY)] * len(weights)
    return pl.pallas_call(
        kernel,
        in_specs=spaces,
        out_specs=[pl.BlockSpec(memory_space=pltpu.VMEM)] * len(outs),
        out_shape=[jax.ShapeDtypeStruct(shape, dtype) for shape, dtype in outs],
        scratch_shapes=list(scratch),
        compiler_params=pltpu.CompilerParams(vmem_limit_bytes=limit * MIB),
        cost_estimate=pl.CostEstimate(flops=0, bytes_accessed=moved, transcendentals=0),
        name=name,
    )(*scalars, *args, *[in_hbm(w) for w in weights])


def start_copies(copies):
    for copy in copies:
        copy.start()


def wait_copies(copies):
    for copy in copies:
        copy.wait()


def row_copies(w_ref, start, held, sems):
    cuts = sems.shape[0]
    rows = held.shape[0] // cuts
    return [
        pltpu.make_async_copy(
            w_ref.at[pl.ds(pl.multiple_of(start + at * rows, 16), rows)],
            held.at[pl.ds(at * rows, rows)],
            sems.at[at],
        )
        for at in range(cuts)
    ]


def column_copies(w_ref, start, held, sems):
    cuts = sems.shape[0]
    rows, width = held.shape
    rows = rows // cuts
    return [
        pltpu.make_async_copy(
            w_ref.at[pl.ds(at * rows, rows), pl.ds(pl.multiple_of(start, 128), width)],
            held.at[pl.ds(at * rows, rows)],
            sems.at[at],
        )
        for at in range(cuts)
    ]


def store_normed(out_ref, x_ref, factor_ref, gain_ref, place):
    width = x_ref.shape[1]
    gain = gain_ref[:, pl.ds(pl.multiple_of(place * width, 128), width)].astype(jnp.float32)
    for c in range(0, width, 128):
        wide = x_ref[:, c : c + 128].astype(jnp.float32)
        out_ref[:, c : c + 128] = (wide * factor_ref[...] * gain[:, c : c + 128]).astype(jnp.bfloat16)


def documents(lengths, docs):
    starts, ends, last = [], [], jnp.int32(0)
    for d in range(docs):
        starts.append(last)
        last = last + lengths[0, d]
        ends.append(last)
    return starts, ends


def by_position(place, for_inner, for_outer):
    return jnp.where((place > 0) & (place < PARTS - 1), for_inner, for_outer)


def early_kernel(
    own, one, two, rest_ref, gain_ref, wq_ref, wkv_ref,
    q_ref, kv_ref, factor_ref, wq_held, wkv_held, normed, sems_q, sems_kv,
):
    place = lax.axis_index("tensor")
    width = own.shape[1]
    shards = (own, one, two)
    spots = (place, place ^ by_position(place, 2, 1), place ^ by_position(place, 1, 2))
    copies = []
    for at in range(len(shards)):
        first, spot = spots[at] * width, pl.ds(at * width, width)
        copies += row_copies(wkv_ref, first, wkv_held.at[spot], sems_kv.at[at])
        copies += row_copies(wq_ref, first, wq_held.at[spot], sems_q.at[at])
    start_copies(copies)
    squares = rest_ref[:, :1]
    for x_ref in shards:
        wide = x_ref[...].astype(jnp.float32)
        squares += jnp.sum(wide * wide, axis=1, keepdims=True)
    factor = lax.rsqrt(squares / (width * (len(shards) + 1)) + EPS)
    factor_ref[...] = jnp.broadcast_to(factor, factor_ref.shape)
    for at, x_ref in enumerate(shards):
        store_normed(normed.at[:, pl.ds(at * width, width)], x_ref, factor_ref, gain_ref, spots[at])
    wait_copies(copies)
    kv_ref[...] = jnp.dot(normed[...], wkv_held[...], preferred_element_type=jnp.float32)
    q_ref[...] = jnp.dot(normed[...], wq_held[...], preferred_element_type=jnp.float32)


def early_projection(own, one, two, rest, gain, wq, wkv):
    rows, width = own.shape
    heads, kv_width = wq.shape[1], wkv.shape[1]
    return resident(
        early_kernel,
        "early_projection",
        [((rows, heads), jnp.float32), ((rows, kv_width), jnp.float32), ((rows, 128), jnp.float32)],
        [own, one, two, rest, gain],
        weights=[wq, wkv],
        scratch=[
            pltpu.VMEM((3 * width, heads), jnp.bfloat16),
            pltpu.VMEM((3 * width, kv_width), jnp.bfloat16),
            pltpu.VMEM((rows, 3 * width), jnp.bfloat16),
            pltpu.SemaphoreType.DMA((3, WEIGHT_CUTS)),
            pltpu.SemaphoreType.DMA((3, 1)),
        ],
        limit=24,
    )


def last_kv_kernel(
    cross, relayed, factor_ref, gain_ref, acc_ref, w_ref, kv_ref, normed, w_held, x, sems
):
    place = lax.axis_index("tensor")
    copies = row_copies(w_ref, (place ^ 3) * x.shape[1], w_held, sems)
    start_copies(copies)
    is_inner = (place > 0) & (place < PARTS - 1)

    @pl.when(is_inner)
    def _():
        store_normed(normed, cross, factor_ref, gain_ref, place ^ 3)

    @pl.when(jnp.logical_not(is_inner))
    def _():
        store_normed(normed, relayed, factor_ref, gain_ref, place ^ 3)

    wait_copies(copies)
    part = jnp.dot(normed[...], w_held[...], preferred_element_type=jnp.float32)
    kv_ref[...] = (acc_ref[...] + part).astype(jnp.bfloat16)


def last_kv(cross, relayed, factor, gain, acc, w):
    rows, columns = acc.shape
    width = relayed.shape[1]
    return resident(
        last_kv_kernel,
        "last_kv",
        [((rows, columns), jnp.bfloat16), ((rows, width), jnp.bfloat16)],
        [cross, relayed, factor, gain, acc],
        weights=[w],
        scratch=[
            pltpu.VMEM((width, columns), jnp.bfloat16),
            pltpu.VMEM((rows, width), jnp.bfloat16),
            pltpu.SemaphoreType.DMA((2,)),
        ],
        limit=8,
    )


def last_q_kernel(normed, acc_ref, w_ref, q_ref, w_held, sems):
    place = lax.axis_index("tensor")
    copies = row_copies(w_ref, (place ^ 3) * normed.shape[1], w_held, sems)
    start_copies(copies)
    wait_copies(copies)
    part = jnp.dot(normed[...], w_held[...], preferred_element_type=jnp.float32)
    q_ref[...] = (acc_ref[...] + part).astype(jnp.bfloat16)


def last_q(normed, acc, w):
    rows, width = normed.shape
    columns = w.shape[1]
    return resident(
        last_q_kernel,
        "last_q",
        [((rows, columns), jnp.bfloat16)],
        [normed, acc],
        weights=[w],
        scratch=[pltpu.VMEM((width, columns), jnp.bfloat16), pltpu.SemaphoreType.DMA((WEIGHT_CUTS,))],
        limit=8,
    )[0]


def attend_kernel(
    row_lengths, cache_lengths, owners, *refs, count, places, sub_rows, heads, divisor
):
    cache, pieces = refs[0], refs[1 : 1 + count]
    q_ref, w_ref, attended_rows, part_ref, held_ref = refs[1 + count : 6 + count]
    w_held, fresh, old_scores, new_scores, top, total, acc, sems, w_sems = refs[6 + count :]
    rank = lax.axis_index("dp")
    place = lax.axis_index("tensor")
    row_count = q_ref.shape[0]
    width = part_ref.shape[1]
    docs = row_lengths.shape[1]
    copies = []
    for at, (piece, own) in enumerate(zip(pieces, places)):
        size = piece.shape[0]
        start = 0 if own is None else (rank if own else 1 - rank) * size
        target = fresh.at[pl.ds(pl.multiple_of(start, 16), size)]
        copies.append(pltpu.make_async_copy(piece, target, sems.at[at]))
    w_copies = column_copies(w_ref, (place ^ 3) * width, w_held, w_sems)
    start_copies(copies + w_copies)

    row_start, row_end = documents(row_lengths, docs)
    cache_start, cache_end = documents(cache_lengths, docs)
    stacked = heads * sub_rows
    lanes = 128

    def by_doc(row, values):
        found = values[0]
        for d in range(1, docs):
            found = jnp.where(row >= row_start[d], values[d], found)
        return found

    pairs = jnp.int32(0)
    for block in range(owners.shape[1]):
        found = jnp.int32(0)
        for d in range(docs):
            low = jnp.maximum(row_start[d], block * BLOCK_ROWS)
            high = jnp.maximum(jnp.minimum(row_end[d], (block + 1) * BLOCK_ROWS), low)
            amount = high - low
            found += amount * (cache_lengths[0, d] + 1 - row_start[d])
            found += lax.shift_right_arithmetic((low + high - 1) * amount, 1)
        pairs += jnp.where(owners[0, block] == rank, found, 0)
    held_ref[...] = jnp.full(held_ref.shape, pairs, jnp.int32).astype(jnp.float32) / divisor

    def span(scores, start, end):
        tile = scores.shape[2]
        start = lax.div(start, 16) * 16
        return start, lax.div(end - start + tile - 1, tile)

    def tile_start(scores, source, first, t):
        tile = scores.shape[2]
        start = first + t * tile
        return start, pl.multiple_of(jnp.minimum(start, source.shape[0] - tile), 16)

    def lane_blocks(values):
        return [values[:, c : c + lanes] for c in range(0, values.shape[1], lanes)]

    for step in range(row_count // sub_rows):
        spots = slice(step * sub_rows, (step + 1) * sub_rows)
        first_row = rank * row_count + step * sub_rows
        last_row = first_row + sub_rows - 1
        rows = first_row + lax.broadcasted_iota(jnp.int32, (sub_rows, 1), 0)
        queries = jnp.concatenate(
            [q_ref[spots, h * HEAD_SIZE : (h + 1) * HEAD_SIZE] for h in range(heads)], axis=0
        )
        top[...] = jnp.full(top.shape, NEG, jnp.float32)
        total[...] = jnp.zeros(total.shape, jnp.float32)
        acc[...] = jnp.zeros(acc.shape, jnp.float32)

        def score(scores, source, first, low, high):
            tile = scores.shape[2]

            def body(t, _):
                begin, start = tile_start(scores, source, first, t)
                found = lax.dot_general(
                    queries,
                    source[pl.ds(start, tile), :HEAD_SIZE],
                    (((1,), (1,)), ((), ())),
                    preferred_element_type=jnp.float32,
                )
                spot = start + lax.broadcasted_iota(jnp.int32, (1, tile), 1)
                seen = (spot >= jnp.maximum(low, begin)) & (spot < high)
                found = jnp.where(seen[None], found.reshape(heads, sub_rows, tile), NEG)
                found = found.reshape(stacked, tile)
                scores[t] = found
                top[...] = functools.reduce(jnp.maximum, lane_blocks(found), top[...])
                return 0

            return body

        cache_from, cache_tiles = span(
            old_scores, by_doc(first_row, cache_start), by_doc(last_row, cache_end)
        )
        new_from, new_tiles = span(new_scores, by_doc(first_row, row_start), last_row + 1)
        low, high = by_doc(rows, cache_start), by_doc(rows, cache_end)
        lax.fori_loop(0, cache_tiles, score(old_scores, cache, cache_from, low, high), 0)
        if step == 0:
            wait_copies(copies)
        low, high = by_doc(rows, row_start), rows + 1
        lax.fori_loop(0, new_tiles, score(new_scores, fresh, new_from, low, high), 0)
        top[...] = jnp.broadcast_to(jnp.max(top[...], axis=1, keepdims=True), top.shape)

        def weigh(scores, source, first):
            tile = scores.shape[2]

            def body(t, _):
                _, start = tile_start(scores, source, first, t)
                highest = top[...]
                weights = [
                    jnp.exp2((scores[t, :, c : c + lanes] - highest) * (HEAD_SIZE**-0.5 * LOG2E))
                    for c in range(0, tile, lanes)
                ]
                total[...] = functools.reduce(jnp.add, weights, total[...])
                acc[...] += jnp.dot(
                    jnp.concatenate([w.astype(jnp.bfloat16) for w in weights], axis=1),
                    source[pl.ds(start, tile), HEAD_SIZE:],
                    preferred_element_type=jnp.float32,
                )
                return 0

            return body

        lax.fori_loop(0, cache_tiles, weigh(old_scores, cache, cache_from), 0)
        lax.fori_loop(0, new_tiles, weigh(new_scores, fresh, new_from), 0)
        attended = (acc[...] / jnp.sum(total[...], axis=1, keepdims=True)).astype(jnp.bfloat16)
        for h in range(heads):
            attended_rows[spots, h * HEAD_SIZE : (h + 1) * HEAD_SIZE] = attended[
                h * sub_rows : (h + 1) * sub_rows
            ]
    wait_copies(w_copies)
    part_ref[...] = jnp.dot(
        attended_rows[...], w_held[...], preferred_element_type=jnp.float32
    ).astype(jnp.bfloat16)


def attention(scalars, queries, cache, pieces, places, fresh, w, divisor):
    rows, width = queries.shape
    heads = width // HEAD_SIZE
    sizes = [(pl.cdiv(cache.shape[0], CACHE_TILE), CACHE_TILE), (pl.cdiv(fresh, NEW_TILE), NEW_TILE)]
    sub_rows = BLOCK_ROWS
    while sub_rows > 32 and heads * sub_rows * 4 * sum(a * b for a, b in sizes) > SCORE_BYTES:
        sub_rows //= 2
    stacked = heads * sub_rows
    out_width = w.shape[1] // PARTS
    return resident(
        functools.partial(
            attend_kernel,
            count=len(pieces),
            places=places,
            sub_rows=sub_rows,
            heads=heads,
            divisor=divisor,
        ),
        "attention",
        [((rows, width), jnp.bfloat16), ((rows, out_width), jnp.bfloat16), ((1, 1), jnp.float32)],
        [cache, *pieces, queries],
        scalars,
        weights=[w],
        scratch=[
            pltpu.VMEM((width, out_width), jnp.bfloat16),
            pltpu.VMEM((fresh, 2 * HEAD_SIZE), jnp.bfloat16),
            *(pltpu.VMEM((tiles, stacked, tile), jnp.float32) for tiles, tile in sizes),
            pltpu.VMEM((stacked, 128), jnp.float32),
            pltpu.VMEM((stacked, 128), jnp.float32),
            pltpu.VMEM((stacked, HEAD_SIZE), jnp.float32),
            pltpu.SemaphoreType.DMA((len(pieces),)),
            pltpu.SemaphoreType.DMA((WEIGHT_CUTS,)),
        ],
        limit=26,
        moved=2 * w.size,
    )


def out_kernel(a_ref, w_ref, one, two, same, w_held, sems):
    outs = (one, two, same)
    place = lax.axis_index("tensor")
    spots = (place ^ by_position(place, 1, 2), place ^ by_position(place, 2, 1), place)
    width = same.shape[1]
    copies = [
        column_copies(w_ref, spot * width, w_held.at[at], sems.at[at]) for at, spot in enumerate(spots)
    ]
    for some in copies:
        start_copies(some)
    for at, out_ref in enumerate(outs):
        wait_copies(copies[at])
        out_ref[...] = jnp.dot(
            a_ref[...], w_held[at], preferred_element_type=jnp.float32
        ).astype(jnp.bfloat16)


def out_projection(attended, w):
    rows, depth = attended.shape
    width = w.shape[1] // PARTS
    return resident(
        out_kernel,
        "out_projection",
        [((rows, width), jnp.bfloat16)] * 3,
        [attended],
        weights=[w],
        scratch=[
            pltpu.VMEM((3, depth, width), jnp.bfloat16),
            pltpu.SemaphoreType.DMA((3, WEIGHT_CUTS)),
        ],
        limit=16,
    )


def on_device(
    tokens, norm_gain, w_query, key_value_weight, w_out, cache_kv, cache_lengths, row_lengths, block_owner
):
    ranks = lax.axis_size("dp")
    splits = lax.axis_size("tensor")
    sections = lax.axis_size("pipe")
    rank = lax.axis_index("dp")
    own = tokens[0]
    row_count = own.shape[0]
    cache_rows = cache_kv.shape[1]
    gain, wq, wkv, wo = norm_gain, w_query[0], key_value_weight[0], w_out[0]
    assert splits == PARTS and row_count % BLOCK_ROWS == 0
    inner_pairs = xor_pairs(splits, 3, range(1, splits - 1))
    pair = [(0, 1), (1, 0)] if ranks == 2 else None

    def onwards(block, pairs):
        route = [
            (p * splits + a, (p + 1) % sections * splits + b) for p in range(sections) for a, b in pairs
        ]
        return swap(block, ("pipe", "tensor"), route)

    one = swap(own, "tensor", [(0, 2), (3, 1), (1, 0), (2, 3)])
    square = jnp.sum(jnp.square(own.astype(jnp.float32)), axis=1)[None]
    rest = swap(square, "tensor", xor_pairs(splits, 3))
    one, rest, late = lax.optimization_barrier((one, rest, own))
    two = swap(late, "tensor", [(0, 1), (3, 2), (1, 3), (2, 0)])
    relayed = swap(one, "tensor", [(1, 0), (2, 3)])
    cross = swap(late, "tensor", inner_pairs)
    cache = after(cache_kv.reshape(cache_rows, 2 * HEAD_SIZE), rest)
    if pair:
        other = swap(cache, "dp", pair)
        cache = jnp.where(
            rank == 0, jnp.concatenate([cache, other]), jnp.concatenate([other, cache])
        )
    else:
        cache = lax.all_gather(cache, "dp", axis=0, tiled=True)

    rest = jnp.broadcast_to(rest[0][:, None], (row_count, 128))
    divisor = BLOCK_ROWS * (cache_rows * ranks // 2 + row_count * ranks // 2)
    early_q, early_kv, factor = early_projection(own, one, two, rest, gain, wq, wkv)
    kv, normed = last_kv(cross, relayed, factor, gain, early_kv, wkv)
    if pair:
        pieces, places = [kv, swap(kv, "dp", pair)], (1, 0)
    else:
        pieces, places = [lax.all_gather(kv, "dp", axis=0, tiled=True)], (None,)
    queries = last_q(normed, early_q, wq)
    home = onwards(after(own, kv), xor_pairs(splits, 0))

    scalars = (row_lengths, cache_lengths, block_owner[:, :, 0])
    attended, third, blocks_held = attention(
        scalars, queries, cache, pieces, places, ranks * row_count, wo, float(divisor)
    )
    from_outer = swap(third, "tensor", [(0, 1), (3, 2)])
    from_cross = onwards(third, inner_pairs)
    attended, home = lax.optimization_barrier((attended, home))
    first, second, same = out_projection(attended, wo)
    from_one = onwards(first, [(0, 2), (3, 1), (1, 0), (2, 3)])
    from_same = onwards(same, xor_pairs(splits, 0))
    summed = (second.astype(jnp.float32) + from_outer.astype(jnp.float32)).astype(jnp.bfloat16)
    from_two = onwards(summed, [(0, 1), (3, 2), (1, 3), (2, 0)])
    total = home.astype(jnp.float32)
    for block in (from_same, from_one, from_cross):
        total = total + block.astype(jnp.float32)
    total = lax.optimization_barrier(total)
    handed = (total + from_two.astype(jnp.float32)).astype(jnp.bfloat16)[None]
    return handed, blocks_held


def solution(mesh):
    placed = (
        P("pipe", "dp", "tensor"),
        P("pipe", None),
        P("pipe", None, "tensor"),
        P("pipe", None, "tensor"),
        P("pipe", "tensor", None),
        P("pipe", "dp", "tensor", None),
        P("pipe", None),
        P("pipe", None),
        P("pipe", None, None),
    )
    return jax.shard_map(
        on_device,
        mesh=mesh,
        in_specs=placed,
        out_specs=(P("pipe", "dp", "tensor"), P("pipe", "dp")),
        check_vma=False,
    )
```

```python
import functools

import jax
import jax.numpy as jnp
from jax import lax
from jax.experimental import pallas as pl
from jax.experimental.pallas import tpu as pltpu
from jax.sharding import PartitionSpec as P

HEAD_SIZE = 128
BLOCK_ROWS = 128
EPS = 1e-06
NEG = -1e30
LOG2E = 1.4426950408889634
MIB = 1024 * 1024
SCORE_BYTES = 13 * MIB
PARTS = 4
WEIGHT_CUTS = 4
CACHE_TILE = 768
NEW_TILE = 512


def swap(block, axis, pairs):
    return lax.ppermute(block, axis, pairs)


def xor_pairs(count, mask, among=None):
    return [(i, i ^ mask) for i in range(count) if among is None or i in among]


def after(value, *others):
    return lax.optimization_barrier((value, *others))[0]


def in_hbm(x):
    return pltpu.with_memory_space_constraint(x, pltpu.HBM)


def resident(kernel, name, outs, args, scalars=(), weights=(), scratch=(), limit=16, moved=0):
    spaces = [pl.BlockSpec(memory_space=pltpu.SMEM)] * len(scalars)
    spaces += [pl.BlockSpec(memory_space=pltpu.VMEM)] * len(args)
    spaces += [pl.BlockSpec(memory_space=pl.ANY)] * len(weights)
    return pl.pallas_call(
        kernel,
        in_specs=spaces,
        out_specs=[pl.BlockSpec(memory_space=pltpu.VMEM)] * len(outs),
        out_shape=[jax.ShapeDtypeStruct(shape, dtype) for shape, dtype in outs],
        scratch_shapes=list(scratch),
        compiler_params=pltpu.CompilerParams(vmem_limit_bytes=limit * MIB),
        cost_estimate=pl.CostEstimate(flops=0, bytes_accessed=moved, transcendentals=0),
        name=name,
    )(*scalars, *args, *[in_hbm(w) for w in weights])


def start_copies(copies):
    for copy in copies:
        copy.start()


def wait_copies(copies):
    for copy in copies:
        copy.wait()


def row_copies(w_ref, start, held, sems):
    cuts = sems.shape[0]
    rows = held.shape[0] // cuts
    return [
        pltpu.make_async_copy(
            w_ref.at[pl.ds(pl.multiple_of(start + at * rows, 16), rows)],
            held.at[pl.ds(at * rows, rows)],
            sems.at[at],
        )
        for at in range(cuts)
    ]


def column_copies(w_ref, start, held, sems):
    cuts = sems.shape[0]
    rows, width = held.shape
    rows = rows // cuts
    return [
        pltpu.make_async_copy(
            w_ref.at[pl.ds(at * rows, rows), pl.ds(pl.multiple_of(start, 128), width)],
            held.at[pl.ds(at * rows, rows)],
            sems.at[at],
        )
        for at in range(cuts)
    ]


def store_normed(out_ref, x_ref, factor_ref, gain_ref, place):
    width = x_ref.shape[1]
    gain = gain_ref[:, pl.ds(pl.multiple_of(place * width, 128), width)].astype(jnp.float32)
    for c in range(0, width, 128):
        wide = x_ref[:, c : c + 128].astype(jnp.float32)
        out_ref[:, c : c + 128] = (wide * factor_ref[...] * gain[:, c : c + 128]).astype(jnp.bfloat16)


def documents(lengths, docs):
    starts, ends, last = [], [], jnp.int32(0)
    for d in range(docs):
        starts.append(last)
        last = last + lengths[0, d]
        ends.append(last)
    return starts, ends


def by_position(place, for_inner, for_outer):
    return jnp.where((place > 0) & (place < PARTS - 1), for_inner, for_outer)


def early_kernel(
    own, one, two, rest_ref, gain_ref, wq_ref, wkv_ref,
    q_ref, kv_ref, factor_ref, wq_held, wkv_held, normed, sems_q, sems_kv,
):
    place = lax.axis_index("tensor")
    width = own.shape[1]
    shards = (own, one, two)
    spots = (place, place ^ by_position(place, 2, 1), place ^ by_position(place, 1, 2))
    copies = []
    for at in range(len(shards)):
        first, spot = spots[at] * width, pl.ds(at * width, width)
        copies += row_copies(wkv_ref, first, wkv_held.at[spot], sems_kv.at[at])
        copies += row_copies(wq_ref, first, wq_held.at[spot], sems_q.at[at])
    start_copies(copies)
    squares = rest_ref[:, :1]
    for x_ref in shards:
        wide = x_ref[...].astype(jnp.float32)
        squares += jnp.sum(wide * wide, axis=1, keepdims=True)
    factor = lax.rsqrt(squares / (width * (len(shards) + 1)) + EPS)
    factor_ref[...] = jnp.broadcast_to(factor, factor_ref.shape)
    for at, x_ref in enumerate(shards):
        store_normed(normed.at[:, pl.ds(at * width, width)], x_ref, factor_ref, gain_ref, spots[at])
    wait_copies(copies)
    kv_ref[...] = jnp.dot(normed[...], wkv_held[...], preferred_element_type=jnp.float32)
    q_ref[...] = jnp.dot(normed[...], wq_held[...], preferred_element_type=jnp.float32)


def early_projection(own, one, two, rest, gain, wq, wkv):
    rows, width = own.shape
    heads, kv_width = wq.shape[1], wkv.shape[1]
    return resident(
        early_kernel,
        "early_projection",
        [((rows, heads), jnp.float32), ((rows, kv_width), jnp.float32), ((rows, 128), jnp.float32)],
        [own, one, two, rest, gain],
        weights=[wq, wkv],
        scratch=[
            pltpu.VMEM((3 * width, heads), jnp.bfloat16),
            pltpu.VMEM((3 * width, kv_width), jnp.bfloat16),
            pltpu.VMEM((rows, 3 * width), jnp.bfloat16),
            pltpu.SemaphoreType.DMA((3, WEIGHT_CUTS)),
            pltpu.SemaphoreType.DMA((3, 1)),
        ],
        limit=24,
    )


def last_kv_kernel(
    cross, relayed, factor_ref, gain_ref, acc_ref, w_ref, kv_ref, normed, w_held, x, sems
):
    place = lax.axis_index("tensor")
    copies = row_copies(w_ref, (place ^ 3) * x.shape[1], w_held, sems)
    start_copies(copies)
    is_inner = (place > 0) & (place < PARTS - 1)

    @pl.when(is_inner)
    def _():
        store_normed(normed, cross, factor_ref, gain_ref, place ^ 3)

    @pl.when(jnp.logical_not(is_inner))
    def _():
        store_normed(normed, relayed, factor_ref, gain_ref, place ^ 3)

    wait_copies(copies)
    part = jnp.dot(normed[...], w_held[...], preferred_element_type=jnp.float32)
    kv_ref[...] = (acc_ref[...] + part).astype(jnp.bfloat16)


def last_kv(cross, relayed, factor, gain, acc, w):
    rows, columns = acc.shape
    width = relayed.shape[1]
    return resident(
        last_kv_kernel,
        "last_kv",
        [((rows, columns), jnp.bfloat16), ((rows, width), jnp.bfloat16)],
        [cross, relayed, factor, gain, acc],
        weights=[w],
        scratch=[
            pltpu.VMEM((width, columns), jnp.bfloat16),
            pltpu.VMEM((rows, width), jnp.bfloat16),
            pltpu.SemaphoreType.DMA((2,)),
        ],
        limit=8,
    )


def last_q_kernel(normed, acc_ref, w_ref, q_ref, w_held, sems):
    place = lax.axis_index("tensor")
    copies = row_copies(w_ref, (place ^ 3) * normed.shape[1], w_held, sems)
    start_copies(copies)
    wait_copies(copies)
    part = jnp.dot(normed[...], w_held[...], preferred_element_type=jnp.float32)
    q_ref[...] = (acc_ref[...] + part).astype(jnp.bfloat16)


def last_q(normed, acc, w):
    rows, width = normed.shape
    columns = w.shape[1]
    return resident(
        last_q_kernel,
        "last_q",
        [((rows, columns), jnp.bfloat16)],
        [normed, acc],
        weights=[w],
        scratch=[pltpu.VMEM((width, columns), jnp.bfloat16), pltpu.SemaphoreType.DMA((WEIGHT_CUTS,))],
        limit=8,
    )[0]


def attend_kernel(
    row_lengths, cache_lengths, owners, *refs, count, places, sub_rows, heads, divisor
):
    cache, pieces = refs[0], refs[1 : 1 + count]
    q_ref, w_ref, attended_rows, part_ref, held_ref = refs[1 + count : 6 + count]
    w_held, fresh, old_scores, new_scores, top, total, acc, sems, w_sems = refs[6 + count :]
    rank = lax.axis_index("dp")
    place = lax.axis_index("tensor")
    row_count = q_ref.shape[0]
    width = part_ref.shape[1]
    docs = row_lengths.shape[1]
    copies = []
    for at, (piece, own) in enumerate(zip(pieces, places)):
        size = piece.shape[0]
        start = 0 if own is None else (rank if own else 1 - rank) * size
        target = fresh.at[pl.ds(pl.multiple_of(start, 16), size)]
        copies.append(pltpu.make_async_copy(piece, target, sems.at[at]))
    w_copies = column_copies(w_ref, (place ^ 3) * width, w_held, w_sems)
    start_copies(copies + w_copies)

    row_start, row_end = documents(row_lengths, docs)
    cache_start, cache_end = documents(cache_lengths, docs)
    stacked = heads * sub_rows
    lanes = 128

    def by_doc(row, values):
        found = values[0]
        for d in range(1, docs):
            found = jnp.where(row >= row_start[d], values[d], found)
        return found

    pairs = jnp.int32(0)
    for block in range(owners.shape[1]):
        found = jnp.int32(0)
        for d in range(docs):
            low = jnp.maximum(row_start[d], block * BLOCK_ROWS)
            high = jnp.maximum(jnp.minimum(row_end[d], (block + 1) * BLOCK_ROWS), low)
            amount = high - low
            found += amount * (cache_lengths[0, d] + 1 - row_start[d])
            found += lax.shift_right_arithmetic((low + high - 1) * amount, 1)
        pairs += jnp.where(owners[0, block] == rank, found, 0)
    held_ref[...] = jnp.full(held_ref.shape, pairs, jnp.int32).astype(jnp.float32) / divisor

    def span(scores, start, end):
        tile = scores.shape[2]
        start = lax.div(start, 16) * 16
        return start, lax.div(end - start + tile - 1, tile)

    def tile_start(scores, source, first, t):
        tile = scores.shape[2]
        start = first + t * tile
        return start, pl.multiple_of(jnp.minimum(start, source.shape[0] - tile), 16)

    def lane_blocks(values):
        return [values[:, c : c + lanes] for c in range(0, values.shape[1], lanes)]

    for step in range(row_count // sub_rows):
        spots = slice(step * sub_rows, (step + 1) * sub_rows)
        first_row = rank * row_count + step * sub_rows
        last_row = first_row + sub_rows - 1
        rows = first_row + lax.broadcasted_iota(jnp.int32, (sub_rows, 1), 0)
        queries = jnp.concatenate(
            [q_ref[spots, h * HEAD_SIZE : (h + 1) * HEAD_SIZE] for h in range(heads)], axis=0
        )
        top[...] = jnp.full(top.shape, NEG, jnp.float32)
        total[...] = jnp.zeros(total.shape, jnp.float32)
        acc[...] = jnp.zeros(acc.shape, jnp.float32)

        def score(scores, source, first, low, high):
            tile = scores.shape[2]

            def body(t, _):
                begin, start = tile_start(scores, source, first, t)
                found = lax.dot_general(
                    queries,
                    source[pl.ds(start, tile), :HEAD_SIZE],
                    (((1,), (1,)), ((), ())),
                    preferred_element_type=jnp.float32,
                )
                spot = start + lax.broadcasted_iota(jnp.int32, (1, tile), 1)
                seen = (spot >= jnp.maximum(low, begin)) & (spot < high)
                found = jnp.where(seen[None], found.reshape(heads, sub_rows, tile), NEG)
                found = found.reshape(stacked, tile)
                scores[t] = found
                top[...] = functools.reduce(jnp.maximum, lane_blocks(found), top[...])
                return 0

            return body

        cache_from, cache_tiles = span(
            old_scores, by_doc(first_row, cache_start), by_doc(last_row, cache_end)
        )
        new_from, new_tiles = span(new_scores, by_doc(first_row, row_start), last_row + 1)
        low, high = by_doc(rows, cache_start), by_doc(rows, cache_end)
        lax.fori_loop(0, cache_tiles, score(old_scores, cache, cache_from, low, high), 0)
        if step == 0:
            wait_copies(copies)
        low, high = by_doc(rows, row_start), rows + 1
        lax.fori_loop(0, new_tiles, score(new_scores, fresh, new_from, low, high), 0)
        top[...] = jnp.broadcast_to(jnp.max(top[...], axis=1, keepdims=True), top.shape)

        def weigh(scores, source, first):
            tile = scores.shape[2]

            def body(t, _):
                _, start = tile_start(scores, source, first, t)
                highest = top[...]
                weights = [
                    jnp.exp2((scores[t, :, c : c + lanes] - highest) * (HEAD_SIZE**-0.5 * LOG2E))
                    for c in range(0, tile, lanes)
                ]
                total[...] = functools.reduce(jnp.add, weights, total[...])
                acc[...] += jnp.dot(
                    jnp.concatenate([w.astype(jnp.bfloat16) for w in weights], axis=1),
                    source[pl.ds(start, tile), HEAD_SIZE:],
                    preferred_element_type=jnp.float32,
                )
                return 0

            return body

        lax.fori_loop(0, cache_tiles, weigh(old_scores, cache, cache_from), 0)
        lax.fori_loop(0, new_tiles, weigh(new_scores, fresh, new_from), 0)
        attended = (acc[...] / jnp.sum(total[...], axis=1, keepdims=True)).astype(jnp.bfloat16)
        for h in range(heads):
            attended_rows[spots, h * HEAD_SIZE : (h + 1) * HEAD_SIZE] = attended[
                h * sub_rows : (h + 1) * sub_rows
            ]
    wait_copies(w_copies)
    part_ref[...] = jnp.dot(
        attended_rows[...], w_held[...], preferred_element_type=jnp.float32
    ).astype(jnp.bfloat16)


def attention(scalars, queries, cache, pieces, places, fresh, w, divisor):
    rows, width = queries.shape
    heads = width // HEAD_SIZE
    sizes = [(pl.cdiv(cache.shape[0], CACHE_TILE), CACHE_TILE), (pl.cdiv(fresh, NEW_TILE), NEW_TILE)]
    sub_rows = BLOCK_ROWS
    while sub_rows > 32 and heads * sub_rows * 4 * sum(a * b for a, b in sizes) > SCORE_BYTES:
        sub_rows //= 2
    stacked = heads * sub_rows
    out_width = w.shape[1] // PARTS
    return resident(
        functools.partial(
            attend_kernel,
            count=len(pieces),
            places=places,
            sub_rows=sub_rows,
            heads=heads,
            divisor=divisor,
        ),
        "attention",
        [((rows, width), jnp.bfloat16), ((rows, out_width), jnp.bfloat16), ((1, 1), jnp.float32)],
        [cache, *pieces, queries],
        scalars,
        weights=[w],
        scratch=[
            pltpu.VMEM((width, out_width), jnp.bfloat16),
            pltpu.VMEM((fresh, 2 * HEAD_SIZE), jnp.bfloat16),
            *(pltpu.VMEM((tiles, stacked, tile), jnp.float32) for tiles, tile in sizes),
            pltpu.VMEM((stacked, 128), jnp.float32),
            pltpu.VMEM((stacked, 128), jnp.float32),
            pltpu.VMEM((stacked, HEAD_SIZE), jnp.float32),
            pltpu.SemaphoreType.DMA((len(pieces),)),
            pltpu.SemaphoreType.DMA((WEIGHT_CUTS,)),
        ],
        limit=26,
        moved=2 * w.size,
    )


def out_kernel(a_ref, w_ref, one, two, same, w_held, sems):
    outs = (one, two, same)
    place = lax.axis_index("tensor")
    spots = (place ^ by_position(place, 1, 2), place ^ by_position(place, 2, 1), place)
    width = same.shape[1]
    copies = [
        column_copies(w_ref, spot * width, w_held.at[at], sems.at[at]) for at, spot in enumerate(spots)
    ]
    for some in copies:
        start_copies(some)
    for at, out_ref in enumerate(outs):
        wait_copies(copies[at])
        out_ref[...] = jnp.dot(
            a_ref[...], w_held[at], preferred_element_type=jnp.float32
        ).astype(jnp.bfloat16)


def out_projection(attended, w):
    rows, depth = attended.shape
    width = w.shape[1] // PARTS
    return resident(
        out_kernel,
        "out_projection",
        [((rows, width), jnp.bfloat16)] * 3,
        [attended],
        weights=[w],
        scratch=[
            pltpu.VMEM((3, depth, width), jnp.bfloat16),
            pltpu.SemaphoreType.DMA((3, WEIGHT_CUTS)),
        ],
        limit=16,
    )


def on_device(
    tokens, norm_gain, w_query, key_value_weight, w_out, cache_kv, cache_lengths, row_lengths, block_owner
):
    ranks = lax.axis_size("dp")
    splits = lax.axis_size("tensor")
    sections = lax.axis_size("pipe")
    rank = lax.axis_index("dp")
    own = tokens[0]
    row_count = own.shape[0]
    cache_rows = cache_kv.shape[1]
    gain, wq, wkv, wo = norm_gain, w_query[0], key_value_weight[0], w_out[0]
    assert splits == PARTS and row_count % BLOCK_ROWS == 0
    inner_pairs = xor_pairs(splits, 3, range(1, splits - 1))
    pair = [(0, 1), (1, 0)] if ranks == 2 else None

    def onwards(block, pairs):
        route = [
            (p * splits + a, (p + 1) % sections * splits + b) for p in range(sections) for a, b in pairs
        ]
        return swap(block, ("pipe", "tensor"), route)

    one = swap(own, "tensor", [(0, 2), (3, 1), (1, 0), (2, 3)])
    square = jnp.sum(jnp.square(own.astype(jnp.float32)), axis=1)[None]
    rest = swap(square, "tensor", xor_pairs(splits, 3))
    one, rest, late = lax.optimization_barrier((one, rest, own))
    two = swap(late, "tensor", [(0, 1), (3, 2), (1, 3), (2, 0)])
    relayed = swap(one, "tensor", [(1, 0), (2, 3)])
    cross = swap(late, "tensor", inner_pairs)
    cache = after(cache_kv.reshape(cache_rows, 2 * HEAD_SIZE), rest)
    if pair:
        other = swap(cache, "dp", pair)
        cache = jnp.where(
            rank == 0, jnp.concatenate([cache, other]), jnp.concatenate([other, cache])
        )
    else:
        cache = lax.all_gather(cache, "dp", axis=0, tiled=True)

    rest = jnp.broadcast_to(rest[0][:, None], (row_count, 128))
    divisor = BLOCK_ROWS * (cache_rows * ranks // 2 + row_count * ranks // 2)
    early_q, early_kv, factor = early_projection(own, one, two, rest, gain, wq, wkv)
    kv, normed = last_kv(cross, relayed, factor, gain, early_kv, wkv)
    if pair:
        pieces, places = [kv, swap(kv, "dp", pair)], (1, 0)
    else:
        pieces, places = [lax.all_gather(kv, "dp", axis=0, tiled=True)], (None,)
    queries = last_q(normed, early_q, wq)
    home = onwards(after(own, kv), xor_pairs(splits, 0))

    scalars = (row_lengths, cache_lengths, block_owner[:, :, 0])
    attended, third, blocks_held = attention(
        scalars, queries, cache, pieces, places, ranks * row_count, wo, float(divisor)
    )
    from_outer = swap(third, "tensor", [(0, 1), (3, 2)])
    from_cross = onwards(third, inner_pairs)
    attended, home = lax.optimization_barrier((attended, home))
    first, second, same = out_projection(attended, wo)
    from_one = onwards(first, [(0, 2), (3, 1), (1, 0), (2, 3)])
    summed = (second.astype(jnp.float32) + from_outer.astype(jnp.float32)).astype(jnp.bfloat16)
    from_two = onwards(summed, [(0, 1), (3, 2), (1, 3), (2, 0)])
    same = lax.optimization_barrier((same, summed))[0]
    from_same = onwards(same, xor_pairs(splits, 0))
    total = home.astype(jnp.float32)
    for block in (from_one, from_cross, from_two):
        total = total + block.astype(jnp.float32)
    total = lax.optimization_barrier(total)
    handed = (total + from_same.astype(jnp.float32)).astype(jnp.bfloat16)[None]
    return handed, blocks_held


def solution(mesh):
    placed = (
        P("pipe", "dp", "tensor"),
        P("pipe", None),
        P("pipe", None, "tensor"),
        P("pipe", None, "tensor"),
        P("pipe", "tensor", None),
        P("pipe", "dp", "tensor", None),
        P("pipe", None),
        P("pipe", None),
        P("pipe", None, None),
    )
    return jax.shard_map(
        on_device,
        mesh=mesh,
        in_specs=placed,
        out_specs=(P("pipe", "dp", "tensor"), P("pipe", "dp")),
        check_vma=False,
    )
```
